32 devices in a mesh: space: 8 (over y, x, core), chan: 4 (over z).
Axes of the slice: x: 2, y: 2, z: 4, core: 2. Of those that a mesh axis runs over, the one named last changes fastest.
Arguments:
- volume: bfloat16 [128, 8, 64, 128], P('chan', 'space'), may hold values from -6 to 6
- weight_one: bfloat16 [27, 128, 128], replicated, may hold values from -0.109375 to 0.109375
- bias_one: float32 [128], replicated, may hold values from -3 to 3
- weight_two: bfloat16 [27, 128, 128], replicated, may hold values from -0.109375 to 0.109375
- bias_two: float32 [128], replicated, may hold values from -3 to 3
Outputs:
- features: bfloat16 [128, 8, 64, 128], P('chan', 'space')
The draws below stay inside these ranges and needn't reach their ends.
All inputs are finite; a program needn't handle non-finite values.
Results may differ from the reference program's by a relative error of at most 0.0045.
Values may be sent and summed in bfloat16 or wider, within the bound.
A program may use at most 64 MiB of HBM per device.

```python
import jax
import jax.numpy as jnp
from jax import lax

C = 128
TAPS = 27
Y = 64
Z = 128
NX = 8


def block_scale(own_key, extent, split, smallest, largest):
    def one(position, parts):
        steps = jax.random.uniform(jax.random.fold_in(jax.random.fold_in(own_key, 6), position), (parts,), jnp.float32, smallest / len(split), largest / len(split))
        return jnp.repeat(jnp.exp(steps), extent[position] // parts).reshape((-1,) + (1,) * (len(extent) - position - 1))

    loudness = one(*split[0])
    for cut in split[1:]:
        loudness = loudness * one(*cut)
    return loudness


def gaussian(own_key, shape, scale, most, shards=(), kind=jnp.bfloat16):
    entries = scale * jax.random.normal(own_key, shape, jnp.float32)
    if shards:
        entries = entries * block_scale(own_key, shape, shards, -0.22, 0.18)
    return jnp.clip(entries, -most, most).astype(kind)


def setup_inputs(seed: int = 0) -> dict:
    seeds = jax.random.split(jax.random.key(seed), 6)
    volume = gaussian(seeds[0], (C, NX, Y, Z), 1.0, 6.0, ((0, 4), (1, 8)))
    weight_one = gaussian(seeds[1], (TAPS, C, C), (TAPS * C) ** -0.5, 0.109375)
    bias_one = gaussian(seeds[2], (C,), 0.5, 3.0, (), jnp.float32)
    weight_two = gaussian(seeds[3], (TAPS, C, C), (TAPS * C) ** -0.5, 0.109375)
    bias_two = gaussian(seeds[4], (C,), 0.5, 3.0, (), jnp.float32)
    return {"volume": volume, "weight_one": weight_one, "bias_one": bias_one, "weight_two": weight_two, "bias_two": bias_two}


def conv_layer(volume, kernel, offsets):
    shaped = kernel.reshape(3, 3, 3, kernel.shape[1], kernel.shape[2]).astype(jnp.float32)
    summed = lax.conv_general_dilated(
        volume[None].astype(jnp.float32), shaped, (1, 1, 1), ((1, 1), (1, 1), (1, 1)),
        dimension_numbers=("NCDHW", "DHWIO", "NCDHW"), precision=lax.Precision.HIGHEST)[0]
    return jax.nn.relu(summed + offsets[:, None, None, None]).astype(jnp.bfloat16)


def reference(volume, weight_one, bias_one, weight_two, bias_two):
    hidden = conv_layer(volume, weight_one, bias_one)
    return conv_layer(hidden, weight_two, bias_two)
```

```python
import functools

import jax
import jax.numpy as jnp
from jax import lax
from jax.experimental import pallas as pl
from jax.experimental.pallas import tpu as pltpu
from jax.sharding import PartitionSpec as P

MESH = pl.DeviceIdType.MESH
BF16 = jnp.bfloat16
F32 = jnp.float32
GROUPS = 4
ORDER_ONE = (0, 1, 3, 2)
ORDER_TWO = (0, 1, 2, 3)


def kernel(ns, nc, rows, depth, own, vol, w1, b1, w2, b2, out,
           field, hidden, result, raw1, raw2, mat1, mat2, bias,
           w_sem, local_sem, z_send, z_recv, x_send, x_recv,
           h_send, h_recv, e_send, e_recv, o_send, o_recv, o_local):
    s = lax.axis_index("space")
    c = lax.axis_index("chan")
    chans = own * nc
    has_lo, has_hi = s > 0, s < ns - 1
    c_lo, c_hi = c > 0, c < nc - 1
    s_dn, s_up = jnp.maximum(s - 1, 0), jnp.minimum(s + 1, ns - 1)
    c_dn, c_up = jnp.maximum(c - 1, 0), jnp.minimum(c + 1, nc - 1)
    peers = [lax.rem(c + k, nc) for k in range(nc)]
    sources = [lax.rem(c + nc - k, nc) for k in range(nc)]
    width = rows * depth
    wide = width + 2 * depth
    group_rows = rows // GROUPS
    group = group_rows * depth
    cut = (rows // 2 + 2) * depth
    halves = ((0, cut), (cut, wide - cut))

    load1 = pltpu.make_async_copy(w1, raw1, w_sem.at[0])
    load2 = pltpu.make_async_copy(w2, raw2, w_sem.at[1])
    load1.start()
    load2.start()

    @pl.when(s == 0)
    def _():
        field[0] = jnp.zeros((chans, wide), BF16)
        hidden[0] = jnp.zeros((chans, wide), BF16)

    @pl.when(s == ns - 1)
    def _():
        field[2] = jnp.zeros((chans, wide), BF16)
        hidden[2] = jnp.zeros((chans, wide), BF16)

    @pl.when(c == 0)
    def _():
        hidden[:, :, 0:depth] = jnp.zeros((3, chans, depth), BF16)

    @pl.when(c == nc - 1)
    def _():
        hidden[:, :, wide - depth : wide] = jnp.zeros((3, chans, depth), BF16)

    barrier = pltpu.get_barrier_semaphore()

    def greet(space, chan):
        pl.semaphore_signal(barrier, inc=1, device_id=(space, chan), device_id_type=MESH)

    for k in range(1, nc):
        greet(s, peers[k])
    for there, space in ((has_lo, s_dn), (has_hi, s_up)):
        @pl.when(there)
        def _(space=space):
            greet(space, c)

        @pl.when(there & c_lo)
        def _(space=space):
            greet(space, c_dn)

        @pl.when(there & c_hi)
        def _(space=space):
            greet(space, c_up)
    sides = has_lo.astype(jnp.int32) + has_hi.astype(jnp.int32)
    edges = c_lo.astype(jnp.int32) + c_hi.astype(jnp.int32)
    pl.semaphore_wait(barrier, nc - 1 + sides * (1 + edges))

    def part(index):
        return pl.ds(pl.multiple_of(index * own, own), own)

    def window(index, half):
        start, size = halves[half]
        return pl.ds(pl.multiple_of(index * width + start, depth), size)

    def landed(half):
        start, size = halves[half]
        return pl.ds(start, size)

    local = [pltpu.make_async_copy(
        vol.at[:, window(c, h)], field.at[1, part(c), landed(h)], local_sem.at[h])
        for h in range(2)]
    to_z = {(k, h): pltpu.make_async_remote_copy(
        src_ref=vol.at[:, window(peers[k], h)],
        dst_ref=field.at[1, part(c), landed(h)],
        send_sem=z_send.at[k - 1, h], recv_sem=z_recv.at[k - 1, h],
        device_id=(s, peers[k]), device_id_type=MESH)
        for h in range(2) for k in range(1, nc)}
    ways = ((0, has_hi, has_lo, s_up, 0), (1, has_lo, has_hi, s_dn, 2))
    to_x = {}
    for d, _, _, space, plane in ways:
        for h in range(2):
            for k in range(nc):
                if k == 0:
                    src = vol.at[:, window(c, h)]
                else:
                    src = field.at[1, part(sources[k]), landed(h)]
                to_x[d, k, h] = pltpu.make_async_remote_copy(
                    src_ref=src,
                    dst_ref=field.at[plane, part(sources[k]), landed(h)],
                    send_sem=x_send.at[d, k, h], recv_sem=x_recv.at[d, k, h],
                    device_id=(space, c), device_id_type=MESH)

    def forward(k, h):
        for d, sends, _, _, _ in ways:
            @pl.when(sends)
            def _(d=d):
                to_x[d, k, h].start()

    for h in range(2):
        for k in range(1, nc):
            to_z[k, h].start()
        local[h].start()
        forward(0, h)

    def turn(raw, mat):
        for ae in range(9):
            for f in range(3):
                mat[f * chans : (f + 1) * chans, ae * chans : (ae + 1) * chans] = raw[3 * ae + f].T

    load1.wait()
    turn(raw1, mat1)
    bias[0] = jnp.broadcast_to(b1[...], (depth, chans)).T
    bias[1] = jnp.broadcast_to(b2[...], (depth, chans)).T

    for k in range(1, nc):
        to_z[k, 0].wait_recv()
        forward(k, 0)
    load2.wait()
    turn(raw2, mat2)
    for k in range(1, nc):
        to_z[k, 1].wait_recv()
        forward(k, 1)

    lane = lax.broadcasted_iota(jnp.int32, (chans, depth), 1)

    def layer(source, mat, layer_bias, g, store):
        @pl.loop(0, group_rows // 2)
        def _(i):
            at = pl.multiple_of(g * group + i * 2 * depth, 2 * depth)
            stacked = jnp.concatenate(
                [source[a, :, pl.ds(pl.multiple_of(at + e * depth, depth), 2 * depth)]
                 for a in range(3) for e in range(3)], axis=0)
            products = jnp.dot(mat[...], stacked, preferred_element_type=F32)
            for r in range(2):
                cols = slice(r * depth, (r + 1) * depth)
                left = pltpu.roll(products[0:chans, cols], 1, 1)
                right = pltpu.roll(products[2 * chans : 3 * chans, cols], depth - 1, 1)
                total = products[chans : 2 * chans, cols] + layer_bias
                total = total + jnp.where(lane == 0, 0.0, left)
                total = total + jnp.where(lane == depth - 1, 0.0, right)
                store(at + r * depth, jnp.maximum(total, 0.0).astype(BF16))

    def keep(at, value):
        hidden[1, :, pl.ds(pl.multiple_of(at + depth, depth), depth)] = value

    def finish(at, value):
        result[:, pl.ds(pl.multiple_of(at, depth), depth)] = value

    to_h = {(d, g): pltpu.make_async_remote_copy(
        src_ref=hidden.at[1, :, pl.ds(depth + g * group, group)],
        dst_ref=hidden.at[plane, :, pl.ds(depth + g * group, group)],
        send_sem=h_send.at[d, g], recv_sem=h_recv.at[d, g],
        device_id=(space, c), device_id_type=MESH)
        for d, _, _, space, plane in ways for g in range(GROUPS)}
    always = s >= 0
    planes = ((0, has_hi, has_lo, s_up, 0), (1, has_lo, has_hi, s_dn, 2), (2, always, always, s, 1))
    rims = ((0, c_lo, c_hi, c_dn, depth, wide - depth), (1, c_hi, c_lo, c_up, width, 0))
    to_e = {(d, t): pltpu.make_async_remote_copy(
        src_ref=hidden.at[1, :, pl.ds(src_at, depth)],
        dst_ref=hidden.at[plane, :, pl.ds(dst_at, depth)],
        send_sem=e_send.at[d, t], recv_sem=e_recv.at[d, t],
        device_id=(space, chan), device_id_type=MESH)
        for d, _, _, space, plane in planes for t, _, _, chan, src_at, dst_at in rims}

    def send_hidden(g):
        for d, sends, _, _, _ in ways:
            @pl.when(sends)
            def _(d=d):
                to_h[d, g].start()
        for t, goes, _, _, _, _ in rims:
            if g == (0, GROUPS - 1)[t]:
                for d, sends, _, _, _ in planes:
                    @pl.when(sends & goes)
                    def _(d=d, t=t):
                        to_e[d, t].start()

    def await_x(h):
        local[h].wait()
        for d, _, comes, _, _ in ways:
            @pl.when(comes)
            def _(d=d):
                for k in range(nc):
                    to_x[d, k, h].wait_recv()

    bias1 = bias[0]
    for step, g in enumerate(ORDER_ONE):
        if step == 0:
            await_x(0)
        if step == GROUPS // 2:
            await_x(1)
        layer(field, mat1, bias1, g, keep)
        send_hidden(g)

    def await_h(g):
        for d, _, comes, _, _ in ways:
            @pl.when(comes)
            def _(d=d):
                to_h[d, g].wait_recv()
        for t, _, lands, _, _, _ in rims:
            if g == (GROUPS - 1, 0)[t]:
                for d, _, comes, _, _ in planes:
                    @pl.when(comes & lands)
                    def _(d=d, t=t):
                        to_e[d, t].wait_recv()

    def piece(g):
        return pl.ds(pl.multiple_of(c * width + g * group, depth), group)

    to_o = {(k, g): pltpu.make_async_remote_copy(
        src_ref=result.at[part(peers[k]), pl.ds(g * group, group)],
        dst_ref=out.at[:, piece(g)],
        send_sem=o_send.at[k - 1, g], recv_sem=o_recv.at[k - 1, g],
        device_id=(s, peers[k]), device_id_type=MESH)
        for k in range(1, nc) for g in range(GROUPS)}
    own_o = [pltpu.make_async_copy(
        result.at[part(c), pl.ds(g * group, group)], out.at[:, piece(g)], o_local.at[g])
        for g in range(GROUPS)]

    bias2 = bias[1]
    seen = set()
    for g in ORDER_TWO:
        for near in (g - 1, g, g + 1):
            if 0 <= near < GROUPS and near not in seen:
                seen.add(near)
                await_h(near)
        layer(hidden, mat2, bias2, g, finish)
        for k in range(1, nc):
            to_o[k, g].start()
        own_o[g].start()

    for (k, h), copy in to_z.items():
        copy.wait_send()
    for d, sends, _, _, _ in ways:
        @pl.when(sends)
        def _(d=d):
            for k in range(nc):
                for h in range(2):
                    to_x[d, k, h].wait_send()
            for g in range(GROUPS):
                to_h[d, g].wait_send()
    for d, sends, _, _, _ in planes:
        for t, goes, _, _, _, _ in rims:
            @pl.when(sends & goes)
            def _(d=d, t=t):
                to_e[d, t].wait_send()
    for copy in to_o.values():
        copy.wait()
    for copy in own_o:
        copy.wait()


def per_device(volume, weight_one, bias_one, weight_two, bias_two):
    own, planes, height, depth = volume.shape
    ns, nc = lax.axis_size("space"), lax.axis_size("chan")
    rows = height // nc
    chans = own * nc
    wide = (rows + 2) * depth
    flat = jnp.pad(volume.reshape(own, height * depth), ((0, 0), (depth, depth)))
    dma = pltpu.SemaphoreType.DMA
    any_space = pl.BlockSpec(memory_space=pl.ANY)
    vmem = pl.BlockSpec(memory_space=pltpu.VMEM)
    macs = 27 * chans * chans * rows * depth
    result = pl.pallas_call(
        functools.partial(kernel, ns, nc, rows, depth, own),
        out_shape=jax.ShapeDtypeStruct((own, height * depth), BF16),
        in_specs=[any_space, any_space, vmem, any_space, vmem],
        out_specs=any_space,
        scratch_shapes=[
            pltpu.VMEM((3, chans, wide), BF16),
            pltpu.VMEM((3, chans, wide), BF16),
            pltpu.VMEM((chans, rows * depth), BF16),
            pltpu.VMEM(weight_one.shape, BF16),
            pltpu.VMEM(weight_two.shape, BF16),
            pltpu.VMEM((3 * chans, 9 * chans), BF16),
            pltpu.VMEM((3 * chans, 9 * chans), BF16),
            pltpu.VMEM((2, chans, depth), F32),
            dma((2,)), dma((2,)),
            dma((nc - 1, 2)), dma((nc - 1, 2)),
            dma((2, nc, 2)), dma((2, nc, 2)),
            dma((2, GROUPS)), dma((2, GROUPS)),
            dma((3, 2)), dma((3, 2)),
            dma((nc - 1, GROUPS)), dma((nc - 1, GROUPS)), dma((GROUPS,)),
        ],
        compiler_params=pltpu.CompilerParams(
            collective_id=0, has_side_effects=True, vmem_limit_bytes=40 * 2**20),
        cost_estimate=pl.CostEstimate(
            flops=4 * macs, bytes_accessed=4 * 2**20, transcendentals=0),
        name="conv_pair",
    )(flat, weight_one, bias_one.reshape(1, chans), weight_two, bias_two.reshape(1, chans))
    return result.reshape(own, planes, height, depth)


def solution(mesh):
    placed = (P("chan", "space", None, None), P(), P(), P(), P())
    return jax.shard_map(
        per_device,
        mesh=mesh,
        in_specs=placed,
        out_specs=P("chan", "space", None, None),
        check_vma=False,
    )
```

```python
import functools

import jax
import jax.numpy as jnp
from jax import lax
from jax.experimental import pallas as pl
from jax.experimental.pallas import tpu as pltpu
from jax.sharding import PartitionSpec as P

MESH = pl.DeviceIdType.MESH
BF16 = jnp.bfloat16
F32 = jnp.float32
PAIR = 2


def row_chunks(rows):
    chunks = [(rows - 2, 4), (0, 4)]
    start = 4
    while start < rows - 2:
        size = min(6, rows - 2 - start)
        chunks.append((start, size))
        start += size
    return chunks


def kernel(ns, nc, rows, depth, own, vol, w1, b1, w2, b2, out,
           field, hidden, result, raw1, raw2, mat1, mat2, bias,
           w_sem, local_sem, z_send, z_recv, x_send, x_recv,
           h_send, h_recv, e_send, e_recv, o_send, o_recv, o_local):
    s = lax.axis_index("space")
    c = lax.axis_index("chan")
    chans = own * nc
    has_lo, has_hi = s > 0, s < ns - 1
    c_lo, c_hi = c > 0, c < nc - 1
    s_dn, s_up = jnp.maximum(s - 1, 0), jnp.minimum(s + 1, ns - 1)
    c_dn, c_up = jnp.maximum(c - 1, 0), jnp.minimum(c + 1, nc - 1)
    peers = [lax.rem(c + k, nc) for k in range(nc)]
    sources = [lax.rem(c + nc - k, nc) for k in range(nc)]
    width = rows * depth
    wide = width + 2 * depth
    groups = rows // PAIR
    group = PAIR * depth
    chunks = row_chunks(rows)
    firsts = [0, 1] + [start // PAIR for start, _ in chunks[2:]]

    load1 = pltpu.make_async_copy(w1, raw1, w_sem.at[0])
    load2 = pltpu.make_async_copy(w2, raw2, w_sem.at[1])
    load1.start()
    load2.start()

    @pl.when(s == 0)
    def _():
        field[0] = jnp.zeros((chans, wide), BF16)
        hidden[0] = jnp.zeros((chans, wide), BF16)

    @pl.when(s == ns - 1)
    def _():
        field[2] = jnp.zeros((chans, wide), BF16)
        hidden[2] = jnp.zeros((chans, wide), BF16)

    @pl.when(c == 0)
    def _():
        hidden[:, :, 0:depth] = jnp.zeros((3, chans, depth), BF16)

    @pl.when(c == nc - 1)
    def _():
        hidden[:, :, wide - depth : wide] = jnp.zeros((3, chans, depth), BF16)

    barrier = pltpu.get_barrier_semaphore()

    def greet(space, chan):
        pl.semaphore_signal(barrier, inc=1, device_id=(space, chan), device_id_type=MESH)

    for k in range(1, nc):
        greet(s, peers[k])
    for there, space in ((has_lo, s_dn), (has_hi, s_up)):
        @pl.when(there)
        def _(space=space):
            greet(space, c)

        @pl.when(there & c_lo)
        def _(space=space):
            greet(space, c_dn)

        @pl.when(there & c_hi)
        def _(space=space):
            greet(space, c_up)
    sides = has_lo.astype(jnp.int32) + has_hi.astype(jnp.int32)
    edges = c_lo.astype(jnp.int32) + c_hi.astype(jnp.int32)
    pl.semaphore_wait(barrier, nc - 1 + sides * (1 + edges))

    def part(index):
        return pl.ds(pl.multiple_of(index * own, own), own)

    def window(index, h):
        start, size = chunks[h]
        return pl.ds(pl.multiple_of(index * width + start * depth, depth), size * depth)

    def landed(h):
        start, size = chunks[h]
        return pl.ds(start * depth, size * depth)

    local = [pltpu.make_async_copy(
        vol.at[:, window(c, h)], field.at[1, part(c), landed(h)], local_sem.at[h])
        for h in range(len(chunks))]
    to_z = {(k, h): pltpu.make_async_remote_copy(
        src_ref=vol.at[:, window(peers[k], h)],
        dst_ref=field.at[1, part(c), landed(h)],
        send_sem=z_send.at[k - 1, h], recv_sem=z_recv.at[k - 1, h],
        device_id=(s, peers[k]), device_id_type=MESH)
        for h in range(len(chunks)) for k in range(1, nc)}
    ways = ((0, has_hi, has_lo, s_up, 0), (1, has_lo, has_hi, s_dn, 2))
    to_x = {}
    for d, _, _, space, plane in ways:
        for h in range(len(chunks)):
            for k in range(nc):
                if k == 0:
                    src = vol.at[:, window(c, h)]
                else:
                    src = field.at[1, part(sources[k]), landed(h)]
                to_x[d, k, h] = pltpu.make_async_remote_copy(
                    src_ref=src,
                    dst_ref=field.at[plane, part(sources[k]), landed(h)],
                    send_sem=x_send.at[d, k, h], recv_sem=x_recv.at[d, k, h],
                    device_id=(space, c), device_id_type=MESH)

    def forward(k, h):
        for d, sends, _, _, _ in ways:
            @pl.when(sends)
            def _(d=d):
                to_x[d, k, h].start()

    def begin(h):
        for k in range(1, nc):
            to_z[k, h].start()
        local[h].start()
        forward(0, h)

    def relay(h):
        for k in range(1, nc):
            to_z[k, h].wait_recv()
            forward(k, h)

    begin(0)
    begin(1)

    def turn(raw, mat, ae_range):
        for ae in ae_range:
            for f in range(3):
                mat[f * chans : (f + 1) * chans, ae * chans : (ae + 1) * chans] = raw[3 * ae + f].T

    load1.wait()
    turn(raw1, mat1, range(9))
    bias[0] = jnp.broadcast_to(b1[...], (depth, chans)).T
    bias[1] = jnp.broadcast_to(b2[...], (depth, chans)).T

    relay(0)
    begin(2)
    load2.wait()
    turn(raw2, mat2, range(3))
    relay(1)
    if len(chunks) > 3:
        begin(3)
    turn(raw2, mat2, range(3, 9))
    relay(2)

    lane = lax.broadcasted_iota(jnp.int32, (chans, depth), 1)

    def layer(source, mat, layer_bias, g, store):
        at = pl.multiple_of(g * group, group)
        stacked = jnp.concatenate(
            [source[a, :, pl.ds(pl.multiple_of(at + e * depth, depth), group)]
             for a in range(3) for e in range(3)], axis=0)
        products = jnp.dot(mat[...], stacked, preferred_element_type=F32)
        for r in range(PAIR):
            cols = slice(r * depth, (r + 1) * depth)
            left = pltpu.roll(products[0:chans, cols], 1, 1)
            right = pltpu.roll(products[2 * chans : 3 * chans, cols], depth - 1, 1)
            total = products[chans : 2 * chans, cols] + layer_bias
            total = total + jnp.where(lane == 0, 0.0, left)
            total = total + jnp.where(lane == depth - 1, 0.0, right)
            store(at + r * depth, jnp.maximum(total, 0.0).astype(BF16))

    def keep(at, value):
        hidden[1, :, pl.ds(pl.multiple_of(at + depth, depth), depth)] = value

    def finish(at, value):
        result[:, pl.ds(pl.multiple_of(at, depth), depth)] = value

    def to_h(d, g):
        space, plane = ways[d][3:]
        cols = pl.ds(pl.multiple_of(g * group + depth, depth), group)
        return pltpu.make_async_remote_copy(
            src_ref=hidden.at[1, :, cols], dst_ref=hidden.at[plane, :, cols],
            send_sem=h_send.at[d, g], recv_sem=h_recv.at[d, g],
            device_id=(space, c), device_id_type=MESH)

    always = s >= 0
    planes = ((0, has_hi, has_lo, s_up, 0), (1, has_lo, has_hi, s_dn, 2), (2, always, always, s, 1))
    rims = ((0, c_lo, c_hi, c_dn, depth, wide - depth), (1, c_hi, c_lo, c_up, width, 0))
    to_e = {(d, t): pltpu.make_async_remote_copy(
        src_ref=hidden.at[1, :, pl.ds(src_at, depth)],
        dst_ref=hidden.at[plane, :, pl.ds(dst_at, depth)],
        send_sem=e_send.at[d, t], recv_sem=e_recv.at[d, t],
        device_id=(space, chan), device_id_type=MESH)
        for d, _, _, space, plane in planes for t, _, _, chan, src_at, dst_at in rims}

    def send_edge(t):
        for d, sends, _, _, _ in planes:
            @pl.when(sends & rims[t][1])
            def _(d=d):
                to_e[d, t].start()

    def await_edge(t):
        for d, _, comes, _, _ in planes:
            @pl.when(comes & rims[t][2])
            def _(d=d):
                to_e[d, t].wait_recv()

    def await_x(h):
        local[h].wait()
        for d, _, comes, _, _ in ways:
            @pl.when(comes)
            def _(d=d):
                for k in range(nc):
                    to_x[d, k, h].wait_recv()

    @pl.loop(0, groups)
    def _(step):
        for h, first in enumerate(firsts):
            @pl.when(step == first)
            def _(h=h):
                if h == 2 and len(chunks) > 3:
                    relay(3)
                await_x(h)

        g = lax.rem(step + groups - 1, groups)
        layer(field, mat1, bias[0], g, keep)

        @pl.when(step == 0)
        def _():
            send_edge(1)

        @pl.when(step == 1)
        def _():
            send_edge(0)

        for d, sends, _, _, _ in ways:
            @pl.when(sends)
            def _(d=d):
                to_h(d, g).start()

    def await_h(g):
        for d, _, comes, _, _ in ways:
            @pl.when(comes)
            def _(d=d):
                to_h(d, g).wait_recv()

    def to_o(k, g):
        here = pl.ds(pl.multiple_of(g * group, group), group)
        there = pl.ds(pl.multiple_of(c * width + g * group, group), group)
        return pltpu.make_async_remote_copy(
            src_ref=result.at[part(peers[k]), here], dst_ref=out.at[:, there],
            send_sem=o_send.at[k - 1, g], recv_sem=o_recv.at[k - 1, g],
            device_id=(s, peers[k]), device_id_type=MESH)

    def own_o(g):
        here = pl.ds(pl.multiple_of(g * group, group), group)
        there = pl.ds(pl.multiple_of(c * width + g * group, group), group)
        return pltpu.make_async_copy(
            result.at[part(c), here], out.at[:, there], o_local.at[g])

    await_h(0)
    await_edge(1)

    @pl.loop(0, groups)
    def _(g):
        @pl.when(g < groups - 1)
        def _():
            await_h(g + 1)

        @pl.when(g == groups - 1)
        def _():
            await_edge(0)

        layer(hidden, mat2, bias[1], g, finish)
        for k in range(1, nc):
            to_o(k, g).start()
        own_o(g).start()

    for (k, h), copy in to_z.items():
        copy.wait_send()
    for d, sends, _, _, _ in ways:
        @pl.when(sends)
        def _(d=d):
            for k in range(nc):
                for h in range(len(chunks)):
                    to_x[d, k, h].wait_send()

            @pl.loop(0, groups)
            def _(g):
                to_h(d, g).wait_send()
    for d, sends, _, _, _ in planes:
        for t, goes, _, _, _, _ in rims:
            @pl.when(sends & goes)
            def _(d=d, t=t):
                to_e[d, t].wait_send()

    @pl.loop(0, groups)
    def _(g):
        for k in range(1, nc):
            to_o(k, g).wait()
        own_o(g).wait()


def per_device(volume, weight_one, bias_one, weight_two, bias_two):
    own, planes, height, depth = volume.shape
    ns, nc = lax.axis_size("space"), lax.axis_size("chan")
    rows = height // nc
    chans = own * nc
    wide = (rows + 2) * depth
    cuts = len(row_chunks(rows))
    flat = jnp.pad(volume.reshape(own, height * depth), ((0, 0), (depth, depth)))
    dma = pltpu.SemaphoreType.DMA
    any_space = pl.BlockSpec(memory_space=pl.ANY)
    vmem = pl.BlockSpec(memory_space=pltpu.VMEM)
    macs = 27 * chans * chans * rows * depth
    result = pl.pallas_call(
        functools.partial(kernel, ns, nc, rows, depth, own),
        out_shape=jax.ShapeDtypeStruct((own, height * depth), BF16),
        in_specs=[any_space, any_space, vmem, any_space, vmem],
        out_specs=any_space,
        scratch_shapes=[
            pltpu.VMEM((3, chans, wide), BF16),
            pltpu.VMEM((3, chans, wide), BF16),
            pltpu.VMEM((chans, rows * depth), BF16),
            pltpu.VMEM(weight_one.shape, BF16),
            pltpu.VMEM(weight_two.shape, BF16),
            pltpu.VMEM((3 * chans, 9 * chans), BF16),
            pltpu.VMEM((3 * chans, 9 * chans), BF16),
            pltpu.VMEM((2, chans, depth), F32),
            dma((2,)), dma((cuts,)),
            dma((nc - 1, cuts)), dma((nc - 1, cuts)),
            dma((2, nc, cuts)), dma((2, nc, cuts)),
            dma((2, rows // PAIR)), dma((2, rows // PAIR)),
            dma((3, 2)), dma((3, 2)),
            dma((nc - 1, rows // PAIR)), dma((nc - 1, rows // PAIR)), dma((rows // PAIR,)),
        ],
        compiler_params=pltpu.CompilerParams(
            collective_id=0, has_side_effects=True, vmem_limit_bytes=40 * 2**20),
        cost_estimate=pl.CostEstimate(
            flops=4 * macs, bytes_accessed=4 * 2**20, transcendentals=0),
        name="conv_pair",
    )(flat, weight_one, bias_one.reshape(1, chans), weight_two, bias_two.reshape(1, chans))
    return result.reshape(own, planes, height, depth)


def solution(mesh):
    placed = (P("chan", "space", None, None), P(), P(), P(), P())
    return jax.shard_map(
        per_device,
        mesh=mesh,
        in_specs=placed,
        out_specs=P("chan", "space", None, None),
        check_vma=False,
    )
```

```python
import functools

import jax
import jax.numpy as jnp
from jax import lax
from jax.experimental import pallas as pl
from jax.experimental.pallas import tpu as pltpu
from jax.sharding import PartitionSpec as P

MESH = pl.DeviceIdType.MESH
BF16 = jnp.bfloat16
F32 = jnp.float32
PAIR = 2


def row_chunks(rows):
    chunks = [(rows - 2, 4), (0, 4)]
    start = 4
    while start < rows - 2:
        size = min(6, rows - 2 - start)
        chunks.append((start, size))
        start += size
    return chunks


def kernel(ns, nc, rows, depth, own, vol, w1, b1, w2, b2, out,
           field, hidden, result, raw1, raw2, mat1, mat2, bias,
           w_sem, local_sem, z_send, z_recv, x_send, x_recv,
           h_send, h_recv, e_send, e_recv, o_send, o_recv, o_local):
    s = lax.axis_index("space")
    c = lax.axis_index("chan")
    chans = own * nc
    has_lo, has_hi = s > 0, s < ns - 1
    c_lo, c_hi = c > 0, c < nc - 1
    s_dn, s_up = jnp.maximum(s - 1, 0), jnp.minimum(s + 1, ns - 1)
    c_dn, c_up = jnp.maximum(c - 1, 0), jnp.minimum(c + 1, nc - 1)
    peers = [lax.rem(c + k, nc) for k in range(nc)]
    sources = [lax.rem(c + nc - k, nc) for k in range(nc)]
    width = rows * depth
    wide = width + 2 * depth
    groups = rows // PAIR
    group = PAIR * depth
    chunks = row_chunks(rows)
    firsts = [0, 1] + [start // PAIR for start, _ in chunks[2:]]

    load1 = pltpu.make_async_copy(w1, raw1, w_sem.at[0])
    load2 = pltpu.make_async_copy(w2, raw2, w_sem.at[1])
    load1.start()
    load2.start()

    @pl.when(s == 0)
    def _():
        field[0] = jnp.zeros((chans, wide), BF16)
        hidden[0] = jnp.zeros((chans, wide), BF16)

    @pl.when(s == ns - 1)
    def _():
        field[2] = jnp.zeros((chans, wide), BF16)
        hidden[2] = jnp.zeros((chans, wide), BF16)

    @pl.when(c == 0)
    def _():
        hidden[:, :, 0:depth] = jnp.zeros((3, chans, depth), BF16)

    @pl.when(c == nc - 1)
    def _():
        hidden[:, :, wide - depth : wide] = jnp.zeros((3, chans, depth), BF16)

    barrier = pltpu.get_barrier_semaphore()

    def greet(space, chan):
        pl.semaphore_signal(barrier, inc=1, device_id=(space, chan), device_id_type=MESH)

    for k in range(1, nc):
        greet(s, peers[k])
    for there, space in ((has_lo, s_dn), (has_hi, s_up)):
        @pl.when(there)
        def _(space=space):
            greet(space, c)

        @pl.when(there & c_lo)
        def _(space=space):
            greet(space, c_dn)

        @pl.when(there & c_hi)
        def _(space=space):
            greet(space, c_up)
    sides = has_lo.astype(jnp.int32) + has_hi.astype(jnp.int32)
    edges = c_lo.astype(jnp.int32) + c_hi.astype(jnp.int32)
    pl.semaphore_wait(barrier, nc - 1 + sides * (1 + edges))

    def part(index):
        return pl.ds(pl.multiple_of(index * own, own), own)

    def window(index, h):
        start, size = chunks[h]
        return pl.ds(pl.multiple_of(index * width + start * depth, depth), size * depth)

    def landed(h):
        start, size = chunks[h]
        return pl.ds(start * depth, size * depth)

    local = [pltpu.make_async_copy(
        vol.at[:, window(c, h)], field.at[1, part(c), landed(h)], local_sem.at[h])
        for h in range(len(chunks))]
    to_z = {(k, h): pltpu.make_async_remote_copy(
        src_ref=vol.at[:, window(peers[k], h)],
        dst_ref=field.at[1, part(c), landed(h)],
        send_sem=z_send.at[k - 1, h], recv_sem=z_recv.at[k - 1, h],
        device_id=(s, peers[k]), device_id_type=MESH)
        for h in range(len(chunks)) for k in range(1, nc)}
    ways = ((0, has_hi, has_lo, s_up, 0), (1, has_lo, has_hi, s_dn, 2))
    to_x = {}
    for d, _, _, space, plane in ways:
        for h in range(len(chunks)):
            for k in range(nc):
                if k == 0:
                    src = vol.at[:, window(c, h)]
                else:
                    src = field.at[1, part(sources[k]), landed(h)]
                to_x[d, k, h] = pltpu.make_async_remote_copy(
                    src_ref=src,
                    dst_ref=field.at[plane, part(sources[k]), landed(h)],
                    send_sem=x_send.at[d, k, h], recv_sem=x_recv.at[d, k, h],
                    device_id=(space, c), device_id_type=MESH)

    def forward(k, h):
        for d, sends, _, _, _ in ways:
            @pl.when(sends)
            def _(d=d):
                to_x[d, k, h].start()

    def begin(h):
        for k in range(1, nc):
            to_z[k, h].start()
        local[h].start()
        forward(0, h)

    def relay(h):
        for k in range(1, nc):
            to_z[k, h].wait_recv()
            forward(k, h)

    begin(0)
    begin(1)

    def turn(raw, mat, ae_range):
        for ae in ae_range:
            for f in range(3):
                mat[f * chans : (f + 1) * chans, ae * chans : (ae + 1) * chans] = raw[3 * ae + f].T

    load1.wait()
    turn(raw1, mat1, range(9))
    bias[0] = jnp.broadcast_to(b1[...], (depth, chans)).T
    bias[1] = jnp.broadcast_to(b2[...], (depth, chans)).T

    relay(0)
    begin(2)
    load2.wait()
    turn(raw2, mat2, range(3))
    relay(1)
    if len(chunks) > 3:
        begin(3)
    turn(raw2, mat2, range(3, 9))
    relay(2)

    lane = lax.broadcasted_iota(jnp.int32, (chans, depth), 1)

    def layer(source, mat, layer_bias, g, store):
        at = pl.multiple_of(g * group, group)
        stacked = jnp.concatenate(
            [source[a, :, pl.ds(pl.multiple_of(at + e * depth, depth), group)]
             for a in range(3) for e in range(3)], axis=0)
        products = jnp.dot(mat[...], stacked, preferred_element_type=F32)
        for r in range(PAIR):
            cols = slice(r * depth, (r + 1) * depth)
            left = pltpu.roll(products[0:chans, cols], 1, 1)
            right = pltpu.roll(products[2 * chans : 3 * chans, cols], depth - 1, 1)
            total = products[chans : 2 * chans, cols] + layer_bias
            total = total + jnp.where(lane == 0, 0.0, left)
            total = total + jnp.where(lane == depth - 1, 0.0, right)
            store(at + r * depth, jnp.maximum(total, 0.0).astype(BF16))

    def keep(at, value):
        hidden[1, :, pl.ds(pl.multiple_of(at + depth, depth), depth)] = value

    def finish(at, value):
        result[:, pl.ds(pl.multiple_of(at, depth), depth)] = value

    def to_h(d, g):
        space, plane = ways[d][3:]
        cols = pl.ds(pl.multiple_of(g * group + depth, depth), group)
        return pltpu.make_async_remote_copy(
            src_ref=hidden.at[1, :, cols], dst_ref=hidden.at[plane, :, cols],
            send_sem=h_send.at[d, g], recv_sem=h_recv.at[d, g],
            device_id=(space, c), device_id_type=MESH)

    always = s >= 0
    planes = ((0, has_hi, has_lo, s_up, 0), (1, has_lo, has_hi, s_dn, 2), (2, always, always, s, 1))
    rims = ((0, c_lo, c_hi, c_dn, depth, wide - depth), (1, c_hi, c_lo, c_up, width, 0))
    to_e = {(d, t): pltpu.make_async_remote_copy(
        src_ref=hidden.at[1, :, pl.ds(src_at, depth)],
        dst_ref=hidden.at[plane, :, pl.ds(dst_at, depth)],
        send_sem=e_send.at[d, t], recv_sem=e_recv.at[d, t],
        device_id=(space, chan), device_id_type=MESH)
        for d, _, _, space, plane in planes for t, _, _, chan, src_at, dst_at in rims}

    def send_edge(t):
        for d, sends, _, _, _ in planes:
            @pl.when(sends & rims[t][1])
            def _(d=d):
                to_e[d, t].start()

    def await_edge(t):
        for d, _, comes, _, _ in planes:
            @pl.when(comes & rims[t][2])
            def _(d=d):
                to_e[d, t].wait_recv()

    def await_x(h):
        local[h].wait()
        for d, _, comes, _, _ in ways:
            @pl.when(comes)
            def _(d=d):
                for k in range(nc):
                    to_x[d, k, h].wait_recv()

    def first_layer(step):
        g = lax.rem(step + groups - 1, groups)
        layer(field, mat1, bias[0], g, keep)

        @pl.when(step == 0)
        def _():
            send_edge(1)

        @pl.when(step == 1)
        def _():
            send_edge(0)

        for d, sends, _, _, _ in ways:
            @pl.when(sends)
            def _(d=d):
                to_h(d, g).start()

    def await_h(g):
        for d, _, comes, _, _ in ways:
            @pl.when(comes)
            def _(d=d):
                to_h(d, g).wait_recv()

    def to_o(k, g):
        here = pl.ds(pl.multiple_of(g * group, group), group)
        there = pl.ds(pl.multiple_of(c * width + g * group, group), group)
        return pltpu.make_async_remote_copy(
            src_ref=result.at[part(peers[k]), here], dst_ref=out.at[:, there],
            send_sem=o_send.at[k - 1, g], recv_sem=o_recv.at[k - 1, g],
            device_id=(s, peers[k]), device_id_type=MESH)

    def own_o(g):
        here = pl.ds(pl.multiple_of(g * group, group), group)
        there = pl.ds(pl.multiple_of(c * width + g * group, group), group)
        return pltpu.make_async_copy(
            result.at[part(c), here], out.at[:, there], o_local.at[g])

    def second_layer(g):
        @pl.when(g == 0)
        def _():
            await_h(0)
            await_edge(1)

        @pl.when(g < groups - 1)
        def _():
            await_h(g + 1)

        @pl.when(g == groups - 1)
        def _():
            await_edge(0)

        layer(hidden, mat2, bias[1], g, finish)
        for k in range(1, nc):
            to_o(k, g).start()
        own_o(g).start()

    late = firsts[3] if len(chunks) > 3 else groups

    @pl.loop(0, late)
    def _(step):
        for h in range(3):
            @pl.when(step == firsts[h])
            def _(h=h):
                await_x(h)

        first_layer(step)

    ahead = 0
    if len(chunks) > 3:
        ahead = late - 3
        relay(3)

        @pl.loop(0, ahead)
        def _(g):
            second_layer(g)

        await_x(3)

        @pl.loop(late, groups)
        def _(step):
            first_layer(step)

    @pl.loop(ahead, groups)
    def _(g):
        second_layer(g)

    for (k, h), copy in to_z.items():
        copy.wait_send()
    for d, sends, _, _, _ in ways:
        @pl.when(sends)
        def _(d=d):
            for k in range(nc):
                for h in range(len(chunks)):
                    to_x[d, k, h].wait_send()

            @pl.loop(0, groups)
            def _(g):
                to_h(d, g).wait_send()
    for d, sends, _, _, _ in planes:
        for t, goes, _, _, _, _ in rims:
            @pl.when(sends & goes)
            def _(d=d, t=t):
                to_e[d, t].wait_send()

    @pl.loop(0, groups)
    def _(g):
        for k in range(1, nc):
            to_o(k, g).wait()
        own_o(g).wait()


def per_device(volume, weight_one, bias_one, weight_two, bias_two):
    own, planes, height, depth = volume.shape
    ns, nc = lax.axis_size("space"), lax.axis_size("chan")
    rows = height // nc
    chans = own * nc
    wide = (rows + 2) * depth
    cuts = len(row_chunks(rows))
    flat = jnp.pad(volume.reshape(own, height * depth), ((0, 0), (depth, depth)))
    dma = pltpu.SemaphoreType.DMA
    any_space = pl.BlockSpec(memory_space=pl.ANY)
    vmem = pl.BlockSpec(memory_space=pltpu.VMEM)
    macs = 27 * chans * chans * rows * depth
    result = pl.pallas_call(
        functools.partial(kernel, ns, nc, rows, depth, own),
        out_shape=jax.ShapeDtypeStruct((own, height * depth), BF16),
        in_specs=[any_space, any_space, vmem, any_space, vmem],
        out_specs=any_space,
        scratch_shapes=[
            pltpu.VMEM((3, chans, wide), BF16),
            pltpu.VMEM((3, chans, wide), BF16),
            pltpu.VMEM((chans, rows * depth), BF16),
            pltpu.VMEM(weight_one.shape, BF16),
            pltpu.VMEM(weight_two.shape, BF16),
            pltpu.VMEM((3 * chans, 9 * chans), BF16),
            pltpu.VMEM((3 * chans, 9 * chans), BF16),
            pltpu.VMEM((2, chans, depth), F32),
            dma((2,)), dma((cuts,)),
            dma((nc - 1, cuts)), dma((nc - 1, cuts)),
            dma((2, nc, cuts)), dma((2, nc, cuts)),
            dma((2, rows // PAIR)), dma((2, rows // PAIR)),
            dma((3, 2)), dma((3, 2)),
            dma((nc - 1, rows // PAIR)), dma((nc - 1, rows // PAIR)), dma((rows // PAIR,)),
        ],
        compiler_params=pltpu.CompilerParams(
            collective_id=0, has_side_effects=True, vmem_limit_bytes=40 * 2**20),
        cost_estimate=pl.CostEstimate(
            flops=4 * macs, bytes_accessed=4 * 2**20, transcendentals=0),
        name="conv_pair",
    )(flat, weight_one, bias_one.reshape(1, chans), weight_two, bias_two.reshape(1, chans))
    return result.reshape(own, planes, height, depth)


def solution(mesh):
    placed = (P("chan", "space", None, None), P(), P(), P(), P())
    return jax.shard_map(
        per_device,
        mesh=mesh,
        in_specs=placed,
        out_specs=P("chan", "space", None, None),
        check_vma=False,
    )
```

```python
import functools

import jax
import jax.numpy as jnp
from jax import lax
from jax.experimental import pallas as pl
from jax.experimental.pallas import tpu as pltpu
from jax.sharding import PartitionSpec as P

MESH = pl.DeviceIdType.MESH
BF16 = jnp.bfloat16
F32 = jnp.float32
GROUP = 4


def row_chunks(rows):
    chunks = [(rows - GROUP, GROUP + 2), (0, min(GROUP + 2, rows - GROUP))]
    for start in range(GROUP + 2, rows - GROUP, GROUP):
        chunks.append((start, min(GROUP, rows - GROUP - start)))
    return chunks


def kernel(ns, nc, rows, depth, own, vol, w1, b1, w2, b2, out,
           field, hidden, result, raw1, raw2, mat1, mat2, bias,
           w_sem, local_sem, z_send, z_recv, x_send, x_recv,
           h_send, h_recv, e_send, e_recv, o_send, o_recv, o_local):
    s = lax.axis_index("space")
    c = lax.axis_index("chan")
    chans = own * nc
    has_lo, has_hi = s > 0, s < ns - 1
    c_lo, c_hi = c > 0, c < nc - 1
    s_dn, s_up = jnp.maximum(s - 1, 0), jnp.minimum(s + 1, ns - 1)
    c_dn, c_up = jnp.maximum(c - 1, 0), jnp.minimum(c + 1, nc - 1)
    peers = [lax.rem(c + k, nc) for k in range(nc)]
    sources = [lax.rem(c + nc - k, nc) for k in range(nc)]
    width = rows * depth
    wide = width + 2 * depth
    groups = rows // GROUP
    group = GROUP * depth
    chunks = row_chunks(rows)
    firsts = list(range(len(chunks)))

    load1 = pltpu.make_async_copy(w1, raw1, w_sem.at[0])
    load2 = pltpu.make_async_copy(w2, raw2, w_sem.at[1])
    load1.start()
    load2.start()

    @pl.when(s == 0)
    def _():
        field[0] = jnp.zeros((chans, wide), BF16)
        hidden[0] = jnp.zeros((chans, wide), BF16)

    @pl.when(s == ns - 1)
    def _():
        field[2] = jnp.zeros((chans, wide), BF16)
        hidden[2] = jnp.zeros((chans, wide), BF16)

    @pl.when(c == 0)
    def _():
        hidden[:, :, 0:depth] = jnp.zeros((3, chans, depth), BF16)

    @pl.when(c == nc - 1)
    def _():
        hidden[:, :, wide - depth : wide] = jnp.zeros((3, chans, depth), BF16)

    barrier = pltpu.get_barrier_semaphore()

    def greet(space, chan):
        pl.semaphore_signal(barrier, inc=1, device_id=(space, chan), device_id_type=MESH)

    for k in range(1, nc):
        greet(s, peers[k])
    for there, space in ((has_lo, s_dn), (has_hi, s_up)):
        @pl.when(there)
        def _(space=space):
            greet(space, c)

        @pl.when(there & c_lo)
        def _(space=space):
            greet(space, c_dn)

        @pl.when(there & c_hi)
        def _(space=space):
            greet(space, c_up)
    sides = has_lo.astype(jnp.int32) + has_hi.astype(jnp.int32)
    edges = c_lo.astype(jnp.int32) + c_hi.astype(jnp.int32)
    pl.semaphore_wait(barrier, nc - 1 + sides * (1 + edges))

    def part(index):
        return pl.ds(pl.multiple_of(index * own, own), own)

    def window(index, h):
        start, size = chunks[h]
        return pl.ds(pl.multiple_of(index * width + start * depth, depth), size * depth)

    def landed(h):
        start, size = chunks[h]
        return pl.ds(start * depth, size * depth)

    local = [pltpu.make_async_copy(
        vol.at[:, window(c, h)], field.at[1, part(c), landed(h)], local_sem.at[h])
        for h in range(len(chunks))]
    to_z = {(k, h): pltpu.make_async_remote_copy(
        src_ref=vol.at[:, window(peers[k], h)],
        dst_ref=field.at[1, part(c), landed(h)],
        send_sem=z_send.at[k - 1, h], recv_sem=z_recv.at[k - 1, h],
        device_id=(s, peers[k]), device_id_type=MESH)
        for h in range(len(chunks)) for k in range(1, nc)}
    ways = ((0, has_hi, has_lo, s_up, 0), (1, has_lo, has_hi, s_dn, 2))
    to_x = {}
    for d, _, _, space, plane in ways:
        for h in range(len(chunks)):
            for k in range(nc):
                if k == 0:
                    src = vol.at[:, window(c, h)]
                else:
                    src = field.at[1, part(sources[k]), landed(h)]
                to_x[d, k, h] = pltpu.make_async_remote_copy(
                    src_ref=src,
                    dst_ref=field.at[plane, part(sources[k]), landed(h)],
                    send_sem=x_send.at[d, k, h], recv_sem=x_recv.at[d, k, h],
                    device_id=(space, c), device_id_type=MESH)

    def forward(k, h):
        for d, sends, _, _, _ in ways:
            @pl.when(sends)
            def _(d=d):
                to_x[d, k, h].start()

    def begin(h):
        for k in range(1, nc):
            to_z[k, h].start()
        local[h].start()
        forward(0, h)

    def relay(h):
        for k in range(1, nc):
            to_z[k, h].wait_recv()
            forward(k, h)

    for h in range(len(chunks)):
        begin(h)

    def turn(raw, mat, ae_range):
        for ae in ae_range:
            for f in range(3):
                mat[f * chans : (f + 1) * chans, ae * chans : (ae + 1) * chans] = raw[3 * ae + f].T

    load1.wait()
    turn(raw1, mat1, range(9))
    bias[0] = jnp.broadcast_to(b1[...], (depth, chans)).T
    bias[1] = jnp.broadcast_to(b2[...], (depth, chans)).T

    relay(0)
    load2.wait()
    turn(raw2, mat2, range(3))
    relay(1)
    turn(raw2, mat2, range(3, 9))

    lane = lax.broadcasted_iota(jnp.int32, (chans, depth), 1)

    def layer(source, mat, layer_bias, g, store):
        at = pl.multiple_of(g * group, group)
        stacked = jnp.concatenate(
            [source[a, :, pl.ds(pl.multiple_of(at + e * depth, depth), group)]
             for a in range(3) for e in range(3)], axis=0)
        products = jnp.dot(mat[...], stacked, preferred_element_type=F32)
        for r in range(GROUP):
            cols = slice(r * depth, (r + 1) * depth)
            left = pltpu.roll(products[0:chans, cols], 1, 1)
            right = pltpu.roll(products[2 * chans : 3 * chans, cols], depth - 1, 1)
            total = products[chans : 2 * chans, cols] + layer_bias
            total = total + jnp.where(lane == 0, 0.0, left)
            total = total + jnp.where(lane == depth - 1, 0.0, right)
            store(at + r * depth, jnp.maximum(total, 0.0).astype(BF16))

    def keep(at, value):
        hidden[1, :, pl.ds(pl.multiple_of(at + depth, depth), depth)] = value

    def finish(at, value):
        result[:, pl.ds(pl.multiple_of(at, depth), depth)] = value

    def to_h(d, g):
        space, plane = ways[d][3:]
        cols = pl.ds(pl.multiple_of(g * group + depth, depth), group)
        return pltpu.make_async_remote_copy(
            src_ref=hidden.at[1, :, cols], dst_ref=hidden.at[plane, :, cols],
            send_sem=h_send.at[d, g], recv_sem=h_recv.at[d, g],
            device_id=(space, c), device_id_type=MESH)

    always = s >= 0
    planes = ((0, has_hi, has_lo, s_up, 0), (1, has_lo, has_hi, s_dn, 2), (2, always, always, s, 1))
    rims = ((0, c_lo, c_hi, c_dn, depth, wide - depth), (1, c_hi, c_lo, c_up, width, 0))
    to_e = {(d, t): pltpu.make_async_remote_copy(
        src_ref=hidden.at[1, :, pl.ds(src_at, depth)],
        dst_ref=hidden.at[plane, :, pl.ds(dst_at, depth)],
        send_sem=e_send.at[d, t], recv_sem=e_recv.at[d, t],
        device_id=(space, chan), device_id_type=MESH)
        for d, _, _, space, plane in planes for t, _, _, chan, src_at, dst_at in rims}

    def send_edge(t):
        for d, sends, _, _, _ in planes:
            @pl.when(sends & rims[t][1])
            def _(d=d):
                to_e[d, t].start()

    def await_edge(t):
        for d, _, comes, _, _ in planes:
            @pl.when(comes & rims[t][2])
            def _(d=d):
                to_e[d, t].wait_recv()

    def await_x(h):
        local[h].wait()
        for d, _, comes, _, _ in ways:
            @pl.when(comes)
            def _(d=d):
                for k in range(nc):
                    to_x[d, k, h].wait_recv()

    @pl.loop(0, groups)
    def _(step):
        for h, first in enumerate(firsts):
            @pl.when(step == first)
            def _(h=h):
                if 0 < h < len(chunks) - 1:
                    relay(h + 1)
                await_x(h)

        g = lax.rem(step + groups - 1, groups)
        layer(field, mat1, bias[0], g, keep)

        @pl.when(step == 0)
        def _():
            send_edge(1)

        @pl.when(step == 1)
        def _():
            send_edge(0)

        for d, sends, _, _, _ in ways:
            @pl.when(sends)
            def _(d=d):
                to_h(d, g).start()

    def await_h(g):
        for d, _, comes, _, _ in ways:
            @pl.when(comes)
            def _(d=d):
                to_h(d, g).wait_recv()

    def to_o(k, g):
        here = pl.ds(pl.multiple_of(g * group, group), group)
        there = pl.ds(pl.multiple_of(c * width + g * group, group), group)
        return pltpu.make_async_remote_copy(
            src_ref=result.at[part(peers[k]), here], dst_ref=out.at[:, there],
            send_sem=o_send.at[k - 1, g], recv_sem=o_recv.at[k - 1, g],
            device_id=(s, peers[k]), device_id_type=MESH)

    def own_o(g):
        here = pl.ds(pl.multiple_of(g * group, group), group)
        there = pl.ds(pl.multiple_of(c * width + g * group, group), group)
        return pltpu.make_async_copy(
            result.at[part(c), here], out.at[:, there], o_local.at[g])

    await_h(0)
    await_edge(1)

    @pl.loop(0, groups)
    def _(g):
        @pl.when(g < groups - 1)
        def _():
            await_h(g + 1)

        @pl.when(g == groups - 1)
        def _():
            await_edge(0)

        layer(hidden, mat2, bias[1], g, finish)
        for k in range(1, nc):
            to_o(k, g).start()
        own_o(g).start()

    for (k, h), copy in to_z.items():
        copy.wait_send()
    for d, sends, _, _, _ in ways:
        @pl.when(sends)
        def _(d=d):
            for k in range(nc):
                for h in range(len(chunks)):
                    to_x[d, k, h].wait_send()

            @pl.loop(0, groups)
            def _(g):
                to_h(d, g).wait_send()
    for d, sends, _, _, _ in planes:
        for t, goes, _, _, _, _ in rims:
            @pl.when(sends & goes)
            def _(d=d, t=t):
                to_e[d, t].wait_send()

    @pl.loop(0, groups)
    def _(g):
        for k in range(1, nc):
            to_o(k, g).wait()
        own_o(g).wait()


def per_device(volume, weight_one, bias_one, weight_two, bias_two):
    own, planes, height, depth = volume.shape
    ns, nc = lax.axis_size("space"), lax.axis_size("chan")
    rows = height // nc
    chans = own * nc
    wide = (rows + 2) * depth
    cuts = len(row_chunks(rows))
    flat = jnp.pad(volume.reshape(own, height * depth), ((0, 0), (depth, depth)))
    dma = pltpu.SemaphoreType.DMA
    any_space = pl.BlockSpec(memory_space=pl.ANY)
    vmem = pl.BlockSpec(memory_space=pltpu.VMEM)
    macs = 27 * chans * chans * rows * depth
    result = pl.pallas_call(
        functools.partial(kernel, ns, nc, rows, depth, own),
        out_shape=jax.ShapeDtypeStruct((own, height * depth), BF16),
        in_specs=[any_space, any_space, vmem, any_space, vmem],
        out_specs=any_space,
        scratch_shapes=[
            pltpu.VMEM((3, chans, wide), BF16),
            pltpu.VMEM((3, chans, wide), BF16),
            pltpu.VMEM((chans, rows * depth), BF16),
            pltpu.VMEM(weight_one.shape, BF16),
            pltpu.VMEM(weight_two.shape, BF16),
            pltpu.VMEM((3 * chans, 9 * chans), BF16),
            pltpu.VMEM((3 * chans, 9 * chans), BF16),
            pltpu.VMEM((2, chans, depth), F32),
            dma((2,)), dma((cuts,)),
            dma((nc - 1, cuts)), dma((nc - 1, cuts)),
            dma((2, nc, cuts)), dma((2, nc, cuts)),
            dma((2, rows // GROUP)), dma((2, rows // GROUP)),
            dma((3, 2)), dma((3, 2)),
            dma((nc - 1, rows // GROUP)), dma((nc - 1, rows // GROUP)), dma((rows // GROUP,)),
        ],
        compiler_params=pltpu.CompilerParams(
            collective_id=0, has_side_effects=True, vmem_limit_bytes=40 * 2**20),
        cost_estimate=pl.CostEstimate(
            flops=4 * macs, bytes_accessed=4 * 2**20, transcendentals=0),
        name="conv_pair",
    )(flat, weight_one, bias_one.reshape(1, chans), weight_two, bias_two.reshape(1, chans))
    return result.reshape(own, planes, height, depth)


def solution(mesh):
    placed = (P("chan", "space", None, None), P(), P(), P(), P())
    return jax.shard_map(
        per_device,
        mesh=mesh,
        in_specs=placed,
        out_specs=P("chan", "space", None, None),
        check_vma=False,
    )
```

```python
import functools

import jax
import jax.numpy as jnp
from jax import lax
from jax.experimental import pallas as pl
from jax.experimental.pallas import tpu as pltpu
from jax.sharding import PartitionSpec as P

MESH = pl.DeviceIdType.MESH
BF16 = jnp.bfloat16
F32 = jnp.float32
PAIR = 2


def row_chunks(rows):
    chunks = [(rows - 2, 4), (0, 4)]
    start = 4
    while start < rows - 2:
        size = min(6, rows - 2 - start)
        chunks.append((start, size))
        start += size
    return chunks


def kernel(ns, nc, rows, depth, own, vol, w1, b1, w2, b2, out,
           field, hidden, result, raw1, raw2, mat1, mat2, bias,
           w_sem, local_sem, z_send, z_recv, x_send, x_recv,
           h_send, h_recv, e_send, e_recv, o_send, o_recv, o_local):
    s = lax.axis_index("space")
    c = lax.axis_index("chan")
    chans = own * nc
    has_lo, has_hi = s > 0, s < ns - 1
    c_lo, c_hi = c > 0, c < nc - 1
    s_dn, s_up = jnp.maximum(s - 1, 0), jnp.minimum(s + 1, ns - 1)
    c_dn, c_up = jnp.maximum(c - 1, 0), jnp.minimum(c + 1, nc - 1)
    peers = [lax.rem(c + k, nc) for k in range(nc)]
    sources = [lax.rem(c + nc - k, nc) for k in range(nc)]
    width = rows * depth
    wide = width + 2 * depth
    groups = rows // PAIR
    group = PAIR * depth
    chunks = row_chunks(rows)
    firsts = [0, 1] + [start // PAIR for start, _ in chunks[2:]]

    load1 = pltpu.make_async_copy(w1, raw1, w_sem.at[0])
    load2 = pltpu.make_async_copy(w2, raw2, w_sem.at[1])
    load1.start()
    load2.start()

    @pl.when(s == 0)
    def _():
        field[0] = jnp.zeros((chans, wide), BF16)
        hidden[0] = jnp.zeros((chans, wide), BF16)

    @pl.when(s == ns - 1)
    def _():
        field[2] = jnp.zeros((chans, wide), BF16)
        hidden[2] = jnp.zeros((chans, wide), BF16)

    @pl.when(c == 0)
    def _():
        hidden[:, :, 0:depth] = jnp.zeros((3, chans, depth), BF16)

    @pl.when(c == nc - 1)
    def _():
        hidden[:, :, wide - depth : wide] = jnp.zeros((3, chans, depth), BF16)

    barrier = pltpu.get_barrier_semaphore()

    def greet(space, chan):
        pl.semaphore_signal(barrier, inc=1, device_id=(space, chan), device_id_type=MESH)

    for k in range(1, nc):
        greet(s, peers[k])
    for there, space in ((has_lo, s_dn), (has_hi, s_up)):
        @pl.when(there)
        def _(space=space):
            greet(space, c)

        @pl.when(there & c_lo)
        def _(space=space):
            greet(space, c_dn)

        @pl.when(there & c_hi)
        def _(space=space):
            greet(space, c_up)
    sides = has_lo.astype(jnp.int32) + has_hi.astype(jnp.int32)
    edges = c_lo.astype(jnp.int32) + c_hi.astype(jnp.int32)
    pl.semaphore_wait(barrier, nc - 1 + sides * (1 + edges))

    def part(index):
        return pl.ds(pl.multiple_of(index * own, own), own)

    def window(index, h):
        start, size = chunks[h]
        return pl.ds(pl.multiple_of(index * width + start * depth, depth), size * depth)

    def landed(h):
        start, size = chunks[h]
        return pl.ds(start * depth, size * depth)

    local = [pltpu.make_async_copy(
        vol.at[:, window(c, h)], field.at[1, part(c), landed(h)], local_sem.at[h])
        for h in range(len(chunks))]
    to_z = {(k, h): pltpu.make_async_remote_copy(
        src_ref=vol.at[:, window(peers[k], h)],
        dst_ref=field.at[1, part(c), landed(h)],
        send_sem=z_send.at[k - 1, h], recv_sem=z_recv.at[k - 1, h],
        device_id=(s, peers[k]), device_id_type=MESH)
        for h in range(len(chunks)) for k in range(1, nc)}
    ways = ((0, has_hi, has_lo, s_up, 0), (1, has_lo, has_hi, s_dn, 2))
    to_x = {}
    for d, _, _, space, plane in ways:
        for h in range(len(chunks)):
            for k in range(nc):
                if k == 0:
                    src = vol.at[:, window(c, h)]
                else:
                    src = field.at[1, part(sources[k]), landed(h)]
                to_x[d, k, h] = pltpu.make_async_remote_copy(
                    src_ref=src,
                    dst_ref=field.at[plane, part(sources[k]), landed(h)],
                    send_sem=x_send.at[d, k, h], recv_sem=x_recv.at[d, k, h],
                    device_id=(space, c), device_id_type=MESH)

    def forward(k, h):
        for d, sends, _, _, _ in ways:
            @pl.when(sends)
            def _(d=d):
                to_x[d, k, h].start()

    def begin(h):
        for k in range(1, nc):
            to_z[k, h].start()
        local[h].start()
        forward(0, h)

    def relay(h):
        for k in range(1, nc):
            to_z[k, h].wait_recv()
            forward(k, h)

    begin(0)
    begin(1)

    unit = jnp.where(
        lax.broadcasted_iota(jnp.int32, (chans, chans), 0)
        == lax.broadcasted_iota(jnp.int32, (chans, chans), 1), 1.0, 0.0).astype(BF16)

    def turn(raw, mat):
        for ae in range(9):
            block = raw[3 * ae : 3 * ae + 3].reshape(3 * chans, chans)
            turned = lax.dot_general(
                unit, block, (((1,), (1,)), ((), ())), preferred_element_type=F32).astype(BF16)
            for f in range(3):
                mat[f * chans : (f + 1) * chans, ae * chans : (ae + 1) * chans] = (
                    turned[:, f * chans : (f + 1) * chans])

    load1.wait()
    turn(raw1, mat1)
    load2.wait()
    turn(raw2, mat2)
    bias[0] = jnp.broadcast_to(b1[...], (depth, chans)).T
    bias[1] = jnp.broadcast_to(b2[...], (depth, chans)).T

    for h in range(2):
        relay(h)
        if h + 2 < len(chunks):
            begin(h + 2)

    lane = lax.broadcasted_iota(jnp.int32, (chans, depth), 1)

    def layer(source, mat, layer_bias, g, store):
        at = pl.multiple_of(g * group, group)
        stacked = jnp.concatenate(
            [source[a, :, pl.ds(pl.multiple_of(at + e * depth, depth), group)]
             for a in range(3) for e in range(3)], axis=0)
        products = jnp.dot(mat[...], stacked, preferred_element_type=F32)
        for r in range(PAIR):
            cols = slice(r * depth, (r + 1) * depth)
            left = pltpu.roll(products[0:chans, cols], 1, 1)
            right = pltpu.roll(products[2 * chans : 3 * chans, cols], depth - 1, 1)
            total = products[chans : 2 * chans, cols] + layer_bias
            total = total + jnp.where(lane == 0, 0.0, left)
            total = total + jnp.where(lane == depth - 1, 0.0, right)
            store(at + r * depth, jnp.maximum(total, 0.0).astype(BF16))

    def keep(at, value):
        hidden[1, :, pl.ds(pl.multiple_of(at + depth, depth), depth)] = value

    def finish(at, value):
        result[:, pl.ds(pl.multiple_of(at, depth), depth)] = value

    def to_h(d, g):
        space, plane = ways[d][3:]
        cols = pl.ds(pl.multiple_of(g * group + depth, depth), group)
        return pltpu.make_async_remote_copy(
            src_ref=hidden.at[1, :, cols], dst_ref=hidden.at[plane, :, cols],
            send_sem=h_send.at[d, g], recv_sem=h_recv.at[d, g],
            device_id=(space, c), device_id_type=MESH)

    always = s >= 0
    planes = ((0, has_hi, has_lo, s_up, 0), (1, has_lo, has_hi, s_dn, 2), (2, always, always, s, 1))
    rims = ((0, c_lo, c_hi, c_dn, depth, wide - depth), (1, c_hi, c_lo, c_up, width, 0))
    to_e = {(d, t): pltpu.make_async_remote_copy(
        src_ref=hidden.at[1, :, pl.ds(src_at, depth)],
        dst_ref=hidden.at[plane, :, pl.ds(dst_at, depth)],
        send_sem=e_send.at[d, t], recv_sem=e_recv.at[d, t],
        device_id=(space, chan), device_id_type=MESH)
        for d, _, _, space, plane in planes for t, _, _, chan, src_at, dst_at in rims}

    def send_edge(t):
        for d, sends, _, _, _ in planes:
            @pl.when(sends & rims[t][1])
            def _(d=d):
                to_e[d, t].start()

    def await_edge(t):
        for d, _, comes, _, _ in planes:
            @pl.when(comes & rims[t][2])
            def _(d=d):
                to_e[d, t].wait_recv()

    def await_x(h):
        local[h].wait()
        for d, _, comes, _, _ in ways:
            @pl.when(comes)
            def _(d=d):
                for k in range(nc):
                    to_x[d, k, h].wait_recv()

    def first_layer(step):
        g = lax.rem(step + groups - 1, groups)
        layer(field, mat1, bias[0], g, keep)

        @pl.when(step == 0)
        def _():
            send_edge(1)

        @pl.when(step == 1)
        def _():
            send_edge(0)

        for d, sends, _, _, _ in ways:
            @pl.when(sends)
            def _(d=d):
                to_h(d, g).start()

    @pl.loop(0, 2)
    def _(step):
        for h in range(2):
            @pl.when(step == h)
            def _(h=h):
                await_x(h)

        first_layer(step)

    for h in range(2, len(chunks)):
        relay(h)

    @pl.loop(2, groups)
    def _(step):
        for h, first in enumerate(firsts):
            if h >= 2:
                @pl.when(step == first)
                def _(h=h):
                    await_x(h)

        first_layer(step)

    def await_h(g):
        for d, _, comes, _, _ in ways:
            @pl.when(comes)
            def _(d=d):
                to_h(d, g).wait_recv()

    def to_o(k, g):
        here = pl.ds(pl.multiple_of(g * group, group), group)
        there = pl.ds(pl.multiple_of(c * width + g * group, group), group)
        return pltpu.make_async_remote_copy(
            src_ref=result.at[part(peers[k]), here], dst_ref=out.at[:, there],
            send_sem=o_send.at[k - 1, g], recv_sem=o_recv.at[k - 1, g],
            device_id=(s, peers[k]), device_id_type=MESH)

    def own_o(g):
        here = pl.ds(pl.multiple_of(g * group, group), group)
        there = pl.ds(pl.multiple_of(c * width + g * group, group), group)
        return pltpu.make_async_copy(
            result.at[part(c), here], out.at[:, there], o_local.at[g])

    await_h(0)
    await_edge(1)

    @pl.loop(0, groups)
    def _(g):
        @pl.when(g < groups - 1)
        def _():
            await_h(g + 1)

        @pl.when(g == groups - 1)
        def _():
            await_edge(0)

        layer(hidden, mat2, bias[1], g, finish)
        for k in range(1, nc):
            to_o(k, g).start()
        own_o(g).start()

    for (k, h), copy in to_z.items():
        copy.wait_send()
    for d, sends, _, _, _ in ways:
        @pl.when(sends)
        def _(d=d):
            for k in range(nc):
                for h in range(len(chunks)):
                    to_x[d, k, h].wait_send()

            @pl.loop(0, groups)
            def _(g):
                to_h(d, g).wait_send()
    for d, sends, _, _, _ in planes:
        for t, goes, _, _, _, _ in rims:
            @pl.when(sends & goes)
            def _(d=d, t=t):
                to_e[d, t].wait_send()

    @pl.loop(0, groups)
    def _(g):
        for k in range(1, nc):
            to_o(k, g).wait()
        own_o(g).wait()


def per_device(volume, weight_one, bias_one, weight_two, bias_two):
    own, planes, height, depth = volume.shape
    ns, nc = lax.axis_size("space"), lax.axis_size("chan")
    rows = height // nc
    chans = own * nc
    wide = (rows + 2) * depth
    cuts = len(row_chunks(rows))
    flat = jnp.pad(volume.reshape(own, height * depth), ((0, 0), (depth, depth)))
    dma = pltpu.SemaphoreType.DMA
    any_space = pl.BlockSpec(memory_space=pl.ANY)
    vmem = pl.BlockSpec(memory_space=pltpu.VMEM)
    macs = 27 * chans * chans * rows * depth
    result = pl.pallas_call(
        functools.partial(kernel, ns, nc, rows, depth, own),
        out_shape=jax.ShapeDtypeStruct((own, height * depth), BF16),
        in_specs=[any_space, any_space, vmem, any_space, vmem],
        out_specs=any_space,
        scratch_shapes=[
            pltpu.VMEM((3, chans, wide), BF16),
            pltpu.VMEM((3, chans, wide), BF16),
            pltpu.VMEM((chans, rows * depth), BF16),
            pltpu.VMEM(weight_one.shape, BF16),
            pltpu.VMEM(weight_two.shape, BF16),
            pltpu.VMEM((3 * chans, 9 * chans), BF16),
            pltpu.VMEM((3 * chans, 9 * chans), BF16),
            pltpu.VMEM((2, chans, depth), F32),
            dma((2,)), dma((cuts,)),
            dma((nc - 1, cuts)), dma((nc - 1, cuts)),
            dma((2, nc, cuts)), dma((2, nc, cuts)),
            dma((2, rows // PAIR)), dma((2, rows // PAIR)),
            dma((3, 2)), dma((3, 2)),
            dma((nc - 1, rows // PAIR)), dma((nc - 1, rows // PAIR)), dma((rows // PAIR,)),
        ],
        compiler_params=pltpu.CompilerParams(
            collective_id=0, has_side_effects=True, vmem_limit_bytes=40 * 2**20),
        cost_estimate=pl.CostEstimate(
            flops=4 * macs, bytes_accessed=4 * 2**20, transcendentals=0),
        name="conv_pair",
    )(flat, weight_one, bias_one.reshape(1, chans), weight_two, bias_two.reshape(1, chans))
    return result.reshape(own, planes, height, depth)


def solution(mesh):
    placed = (P("chan", "space", None, None), P(), P(), P(), P())
    return jax.shard_map(
        per_device,
        mesh=mesh,
        in_specs=placed,
        out_specs=P("chan", "space", None, None),
        check_vma=False,
    )
```

```python
import functools

import jax
import jax.numpy as jnp
from jax import lax
from jax.experimental import pallas as pl
from jax.experimental.pallas import tpu as pltpu
from jax.sharding import PartitionSpec as P

MESH = pl.DeviceIdType.MESH
BF16 = jnp.bfloat16
F32 = jnp.float32
PAIR = 2


def row_chunks(rows):
    chunks = [(rows - 2, 4), (0, 4)]
    start = 4
    while start < rows - 2:
        size = min(6, rows - 2 - start)
        chunks.append((start, size))
        start += size
    return chunks


def kernel(ns, nc, rows, depth, own, vol, w1, b1, w2, b2, out,
           field, hidden, result, raw1, raw2, mat1, mat2, bias, raw_bias,
           w_sem, local_sem, z_send, z_recv, x_send, x_recv,
           h_send, h_recv, e_send, e_recv, o_send, o_recv, o_local):
    s = lax.axis_index("space")
    c = lax.axis_index("chan")
    chans = own * nc
    has_lo, has_hi = s > 0, s < ns - 1
    c_lo, c_hi = c > 0, c < nc - 1
    s_dn, s_up = jnp.maximum(s - 1, 0), jnp.minimum(s + 1, ns - 1)
    c_dn, c_up = jnp.maximum(c - 1, 0), jnp.minimum(c + 1, nc - 1)
    peers = [lax.rem(c + k, nc) for k in range(nc)]
    sources = [lax.rem(c + nc - k, nc) for k in range(nc)]
    width = rows * depth
    wide = width + 2 * depth
    groups = rows // PAIR
    group = PAIR * depth
    chunks = row_chunks(rows)
    firsts = [0, 1] + [start // PAIR for start, _ in chunks[2:]]

    load1 = pltpu.make_async_copy(w1, raw1, w_sem.at[0])
    load2 = pltpu.make_async_copy(w2, raw2, w_sem.at[1])
    load3 = pltpu.make_async_copy(b1, raw_bias.at[0], w_sem.at[2])
    load4 = pltpu.make_async_copy(b2, raw_bias.at[1], w_sem.at[3])
    load1.start()
    load2.start()
    load3.start()
    load4.start()

    @pl.when(s == 0)
    def _():
        field[0] = jnp.zeros((chans, wide), BF16)
        hidden[0] = jnp.zeros((chans, wide), BF16)

    @pl.when(s == ns - 1)
    def _():
        field[2] = jnp.zeros((chans, wide), BF16)
        hidden[2] = jnp.zeros((chans, wide), BF16)

    @pl.when(c == 0)
    def _():
        hidden[:, :, 0:depth] = jnp.zeros((3, chans, depth), BF16)

    @pl.when(c == nc - 1)
    def _():
        hidden[:, :, wide - depth : wide] = jnp.zeros((3, chans, depth), BF16)

    barrier = pltpu.get_barrier_semaphore()

    def greet(space, chan):
        pl.semaphore_signal(barrier, inc=1, device_id=(space, chan), device_id_type=MESH)

    for k in range(1, nc):
        greet(s, peers[k])
    for there, space in ((has_lo, s_dn), (has_hi, s_up)):
        @pl.when(there)
        def _(space=space):
            greet(space, c)

        @pl.when(there & c_lo)
        def _(space=space):
            greet(space, c_dn)

        @pl.when(there & c_hi)
        def _(space=space):
            greet(space, c_up)
    sides = has_lo.astype(jnp.int32) + has_hi.astype(jnp.int32)
    edges = c_lo.astype(jnp.int32) + c_hi.astype(jnp.int32)
    pl.semaphore_wait(barrier, nc - 1 + sides * (1 + edges))

    def part(index):
        return pl.ds(pl.multiple_of(index * own, own), own)

    def window(index, h):
        start, size = chunks[h]
        return pl.ds(pl.multiple_of(index * width + start * depth, depth), size * depth)

    def landed(h):
        start, size = chunks[h]
        return pl.ds(start * depth, size * depth)

    local = [pltpu.make_async_copy(
        vol.at[:, window(c, h)], field.at[1, part(c), landed(h)], local_sem.at[h])
        for h in range(len(chunks))]
    to_z = {(k, h): pltpu.make_async_remote_copy(
        src_ref=vol.at[:, window(peers[k], h)],
        dst_ref=field.at[1, part(c), landed(h)],
        send_sem=z_send.at[k - 1, h], recv_sem=z_recv.at[k - 1, h],
        device_id=(s, peers[k]), device_id_type=MESH)
        for h in range(len(chunks)) for k in range(1, nc)}
    ways = ((0, has_hi, has_lo, s_up, 0), (1, has_lo, has_hi, s_dn, 2))
    to_x = {}
    for d, _, _, space, plane in ways:
        for h in range(len(chunks)):
            for k in range(nc):
                if k == 0:
                    src = vol.at[:, window(c, h)]
                else:
                    src = field.at[1, part(sources[k]), landed(h)]
                to_x[d, k, h] = pltpu.make_async_remote_copy(
                    src_ref=src,
                    dst_ref=field.at[plane, part(sources[k]), landed(h)],
                    send_sem=x_send.at[d, k, h], recv_sem=x_recv.at[d, k, h],
                    device_id=(space, c), device_id_type=MESH)

    def forward(k, h):
        for d, sends, _, _, _ in ways:
            @pl.when(sends)
            def _(d=d):
                to_x[d, k, h].start()

    def begin(h):
        for k in range(1, nc):
            to_z[k, h].start()
        local[h].start()
        forward(0, h)

    def relay(h):
        for k in range(1, nc):
            to_z[k, h].wait_recv()
            forward(k, h)

    for h in range(len(chunks)):
        begin(h)

    unit = jnp.where(
        lax.broadcasted_iota(jnp.int32, (chans, chans), 0)
        == lax.broadcasted_iota(jnp.int32, (chans, chans), 1), 1.0, 0.0).astype(BF16)

    def turn(raw, mat):
        for ae in range(9):
            block = raw[3 * ae : 3 * ae + 3].reshape(3 * chans, chans)
            turned = lax.dot_general(
                unit, block, (((1,), (1,)), ((), ())), preferred_element_type=F32).astype(BF16)
            for f in range(3):
                mat[f * chans : (f + 1) * chans, ae * chans : (ae + 1) * chans] = (
                    turned[:, f * chans : (f + 1) * chans])

    load1.wait()
    turn(raw1, mat1)
    load2.wait()
    turn(raw2, mat2)
    load3.wait()
    load4.wait()
    bias[0] = jnp.broadcast_to(raw_bias[0], (depth, chans)).T
    bias[1] = jnp.broadcast_to(raw_bias[1], (depth, chans)).T

    for h in range(2):
        relay(h)

    lane = lax.broadcasted_iota(jnp.int32, (chans, depth), 1)

    def layer(source, mat, layer_bias, g, store):
        at = pl.multiple_of(g * group, group)
        stacked = jnp.concatenate(
            [source[a, :, pl.ds(pl.multiple_of(at + e * depth, depth), group)]
             for a in range(3) for e in range(3)], axis=0)
        products = jnp.dot(mat[...], stacked, preferred_element_type=F32)
        for r in range(PAIR):
            cols = slice(r * depth, (r + 1) * depth)
            left = pltpu.roll(products[0:chans, cols], 1, 1)
            right = pltpu.roll(products[2 * chans : 3 * chans, cols], depth - 1, 1)
            total = products[chans : 2 * chans, cols] + layer_bias
            total = total + jnp.where(lane == 0, 0.0, left)
            total = total + jnp.where(lane == depth - 1, 0.0, right)
            store(at + r * depth, jnp.maximum(total, 0.0).astype(BF16))

    def keep(at, value):
        hidden[1, :, pl.ds(pl.multiple_of(at + depth, depth), depth)] = value

    def finish(at, value):
        result[:, pl.ds(pl.multiple_of(at, depth), depth)] = value

    def to_h(d, g):
        space, plane = ways[d][3:]
        cols = pl.ds(pl.multiple_of(g * group + depth, depth), group)
        return pltpu.make_async_remote_copy(
            src_ref=hidden.at[1, :, cols], dst_ref=hidden.at[plane, :, cols],
            send_sem=h_send.at[d, g], recv_sem=h_recv.at[d, g],
            device_id=(space, c), device_id_type=MESH)

    always = s >= 0
    planes = ((0, has_hi, has_lo, s_up, 0), (1, has_lo, has_hi, s_dn, 2), (2, always, always, s, 1))
    rims = ((0, c_lo, c_hi, c_dn, depth, wide - depth), (1, c_hi, c_lo, c_up, width, 0))
    to_e = {(d, t): pltpu.make_async_remote_copy(
        src_ref=hidden.at[1, :, pl.ds(src_at, depth)],
        dst_ref=hidden.at[plane, :, pl.ds(dst_at, depth)],
        send_sem=e_send.at[d, t], recv_sem=e_recv.at[d, t],
        device_id=(space, chan), device_id_type=MESH)
        for d, _, _, space, plane in planes for t, _, _, chan, src_at, dst_at in rims}

    def send_edge(t):
        for d, sends, _, _, _ in planes:
            @pl.when(sends & rims[t][1])
            def _(d=d):
                to_e[d, t].start()

    def await_edge(t):
        for d, _, comes, _, _ in planes:
            @pl.when(comes & rims[t][2])
            def _(d=d):
                to_e[d, t].wait_recv()

    def await_x(h):
        local[h].wait()
        for d, _, comes, _, _ in ways:
            @pl.when(comes)
            def _(d=d):
                for k in range(nc):
                    to_x[d, k, h].wait_recv()

    def first_layer(step):
        g = lax.rem(step + groups - 1, groups)
        layer(field, mat1, bias[0], g, keep)

        @pl.when(step == 0)
        def _():
            send_edge(1)

        @pl.when(step == 1)
        def _():
            send_edge(0)

        for d, sends, _, _, _ in ways:
            @pl.when(sends)
            def _(d=d):
                to_h(d, g).start()

    @pl.loop(0, 2)
    def _(step):
        for h in range(2):
            @pl.when(step == h)
            def _(h=h):
                await_x(h)

        first_layer(step)

    for h in range(2, len(chunks)):
        relay(h)

    @pl.loop(2, groups)
    def _(step):
        for h, first in enumerate(firsts):
            if h >= 2:
                @pl.when(step == first)
                def _(h=h):
                    await_x(h)

        first_layer(step)

    def await_h(g):
        for d, _, comes, _, _ in ways:
            @pl.when(comes)
            def _(d=d):
                to_h(d, g).wait_recv()

    def to_o(k, g):
        here = pl.ds(pl.multiple_of(g * group, group), group)
        there = pl.ds(pl.multiple_of(c * width + g * group, group), group)
        return pltpu.make_async_remote_copy(
            src_ref=result.at[part(peers[k]), here], dst_ref=out.at[:, there],
            send_sem=o_send.at[k - 1, g], recv_sem=o_recv.at[k - 1, g],
            device_id=(s, peers[k]), device_id_type=MESH)

    def own_o(g):
        here = pl.ds(pl.multiple_of(g * group, group), group)
        there = pl.ds(pl.multiple_of(c * width + g * group, group), group)
        return pltpu.make_async_copy(
            result.at[part(c), here], out.at[:, there], o_local.at[g])

    await_h(0)
    await_edge(1)

    @pl.loop(0, groups)
    def _(g):
        @pl.when(g < groups - 1)
        def _():
            await_h(g + 1)

        @pl.when(g == groups - 1)
        def _():
            await_edge(0)

        layer(hidden, mat2, bias[1], g, finish)
        for k in range(1, nc):
            to_o(k, g).start()
        own_o(g).start()

    for (k, h), copy in to_z.items():
        copy.wait_send()
    for d, sends, _, _, _ in ways:
        @pl.when(sends)
        def _(d=d):
            for k in range(nc):
                for h in range(len(chunks)):
                    to_x[d, k, h].wait_send()

            @pl.loop(0, groups)
            def _(g):
                to_h(d, g).wait_send()
    for d, sends, _, _, _ in planes:
        for t, goes, _, _, _, _ in rims:
            @pl.when(sends & goes)
            def _(d=d, t=t):
                to_e[d, t].wait_send()

    @pl.loop(0, groups)
    def _(g):
        for k in range(1, nc):
            to_o(k, g).wait()
        own_o(g).wait()


def per_device(volume, weight_one, bias_one, weight_two, bias_two):
    own, planes, height, depth = volume.shape
    ns, nc = lax.axis_size("space"), lax.axis_size("chan")
    rows = height // nc
    chans = own * nc
    wide = (rows + 2) * depth
    cuts = len(row_chunks(rows))
    flat = jnp.pad(volume.reshape(own, height * depth), ((0, 0), (depth, depth)))
    dma = pltpu.SemaphoreType.DMA
    any_space = pl.BlockSpec(memory_space=pl.ANY)
    macs = 27 * chans * chans * rows * depth
    result = pl.pallas_call(
        functools.partial(kernel, ns, nc, rows, depth, own),
        out_shape=jax.ShapeDtypeStruct((own, height * depth), BF16),
        in_specs=[any_space] * 5,
        out_specs=any_space,
        scratch_shapes=[
            pltpu.VMEM((3, chans, wide), BF16),
            pltpu.VMEM((3, chans, wide), BF16),
            pltpu.VMEM((chans, rows * depth), BF16),
            pltpu.VMEM(weight_one.shape, BF16),
            pltpu.VMEM(weight_two.shape, BF16),
            pltpu.VMEM((3 * chans, 9 * chans), BF16),
            pltpu.VMEM((3 * chans, 9 * chans), BF16),
            pltpu.VMEM((2, chans, depth), F32),
            pltpu.VMEM((2, 1, chans), F32),
            dma((4,)), dma((cuts,)),
            dma((nc - 1, cuts)), dma((nc - 1, cuts)),
            dma((2, nc, cuts)), dma((2, nc, cuts)),
            dma((2, rows // PAIR)), dma((2, rows // PAIR)),
            dma((3, 2)), dma((3, 2)),
            dma((nc - 1, rows // PAIR)), dma((nc - 1, rows // PAIR)), dma((rows // PAIR,)),
        ],
        compiler_params=pltpu.CompilerParams(
            collective_id=0, has_side_effects=True, vmem_limit_bytes=40 * 2**20),
        cost_estimate=pl.CostEstimate(
            flops=4 * macs, bytes_accessed=4 * 2**20, transcendentals=0),
        name="conv_pair",
    )(flat, weight_one, bias_one.reshape(1, chans), weight_two, bias_two.reshape(1, chans))
    return result.reshape(own, planes, height, depth)


def solution(mesh):
    placed = (P("chan", "space", None, None), P(), P(), P(), P())
    return jax.shard_map(
        per_device,
        mesh=mesh,
        in_specs=placed,
        out_specs=P("chan", "space", None, None),
        check_vma=False,
    )
```

```python
import functools

import jax
import jax.numpy as jnp
from jax import lax
from jax.experimental import pallas as pl
from jax.experimental.pallas import tpu as pltpu
from jax.sharding import PartitionSpec as P

MESH = pl.DeviceIdType.MESH
BF16 = jnp.bfloat16
F32 = jnp.float32
PAIR = 2


def row_chunks(rows):
    chunks = [(rows - 2, 4), (0, 4)]
    start = 4
    while start < rows - 2:
        size = min(6, rows - 2 - start)
        chunks.append((start, size))
        start += size
    return chunks


def kernel(ns, nc, rows, depth, own, vol, w1, b1, w2, b2, out,
           field, hidden, result, raw1, raw2, mat1, mat2, bias,
           w_sem, local_sem, z_send, z_recv, x_send, x_recv,
           h_send, h_recv, e_send, e_recv, o_send, o_recv, o_local):
    s = lax.axis_index("space")
    c = lax.axis_index("chan")
    chans = own * nc
    has_lo, has_hi = s > 0, s < ns - 1
    c_lo, c_hi = c > 0, c < nc - 1
    s_dn, s_up = jnp.maximum(s - 1, 0), jnp.minimum(s + 1, ns - 1)
    c_dn, c_up = jnp.maximum(c - 1, 0), jnp.minimum(c + 1, nc - 1)
    peers = [lax.rem(c + k, nc) for k in range(nc)]
    near_first = sorted(range(1, nc), key=lambda k: min(k, nc - k))
    sources = [lax.rem(c + nc - k, nc) for k in range(nc)]
    width = rows * depth
    wide = width + 2 * depth
    groups = rows // PAIR
    group = PAIR * depth
    chunks = row_chunks(rows)
    firsts = [0, 1] + [start // PAIR for start, _ in chunks[2:]]

    load1 = pltpu.make_async_copy(w1, raw1, w_sem.at[0])
    load2 = pltpu.make_async_copy(w2, raw2, w_sem.at[1])
    load1.start()
    load2.start()

    @pl.when(s == 0)
    def _():
        field[0] = jnp.zeros((chans, wide), BF16)
        hidden[0] = jnp.zeros((chans, wide), BF16)

    @pl.when(s == ns - 1)
    def _():
        field[2] = jnp.zeros((chans, wide), BF16)
        hidden[2] = jnp.zeros((chans, wide), BF16)

    @pl.when(c == 0)
    def _():
        hidden[:, :, 0:depth] = jnp.zeros((3, chans, depth), BF16)

    @pl.when(c == nc - 1)
    def _():
        hidden[:, :, wide - depth : wide] = jnp.zeros((3, chans, depth), BF16)

    barrier = pltpu.get_barrier_semaphore()

    def greet(space, chan):
        pl.semaphore_signal(barrier, inc=1, device_id=(space, chan), device_id_type=MESH)

    for k in range(1, nc):
        greet(s, peers[k])
    for there, space in ((has_lo, s_dn), (has_hi, s_up)):
        @pl.when(there)
        def _(space=space):
            greet(space, c)

        @pl.when(there & c_lo)
        def _(space=space):
            greet(space, c_dn)

        @pl.when(there & c_hi)
        def _(space=space):
            greet(space, c_up)
    sides = has_lo.astype(jnp.int32) + has_hi.astype(jnp.int32)
    edges = c_lo.astype(jnp.int32) + c_hi.astype(jnp.int32)
    pl.semaphore_wait(barrier, nc - 1 + sides * (1 + edges))

    def part(index):
        return pl.ds(pl.multiple_of(index * own, own), own)

    def window(index, h):
        start, size = chunks[h]
        return pl.ds(pl.multiple_of(index * width + start * depth, depth), size * depth)

    def landed(h):
        start, size = chunks[h]
        return pl.ds(start * depth, size * depth)

    local = [pltpu.make_async_copy(
        vol.at[:, window(c, h)], field.at[1, part(c), landed(h)], local_sem.at[h])
        for h in range(len(chunks))]
    to_z = {(k, h): pltpu.make_async_remote_copy(
        src_ref=vol.at[:, window(peers[k], h)],
        dst_ref=field.at[1, part(c), landed(h)],
        send_sem=z_send.at[k - 1, h], recv_sem=z_recv.at[k - 1, h],
        device_id=(s, peers[k]), device_id_type=MESH)
        for h in range(len(chunks)) for k in range(1, nc)}
    ways = ((0, has_hi, has_lo, s_up, 0), (1, has_lo, has_hi, s_dn, 2))
    to_x = {}
    for d, _, _, space, plane in ways:
        for h in range(len(chunks)):
            for k in range(nc):
                if k == 0:
                    src = vol.at[:, window(c, h)]
                else:
                    src = field.at[1, part(sources[k]), landed(h)]
                to_x[d, k, h] = pltpu.make_async_remote_copy(
                    src_ref=src,
                    dst_ref=field.at[plane, part(sources[k]), landed(h)],
                    send_sem=x_send.at[d, k, h], recv_sem=x_recv.at[d, k, h],
                    device_id=(space, c), device_id_type=MESH)

    def forward(k, h):
        for d, sends, _, _, _ in ways:
            @pl.when(sends)
            def _(d=d):
                to_x[d, k, h].start()

    def begin(h):
        for k in range(1, nc):
            to_z[k, h].start()
        local[h].start()
        forward(0, h)

    def relay(h):
        for k in near_first:
            to_z[k, h].wait_recv()
            forward(k, h)

    begin(0)
    begin(1)

    unit = jnp.where(
        lax.broadcasted_iota(jnp.int32, (chans, chans), 0)
        == lax.broadcasted_iota(jnp.int32, (chans, chans), 1), 1.0, 0.0).astype(BF16)

    def turn(raw, mat):
        for ae in range(9):
            block = raw[3 * ae : 3 * ae + 3].reshape(3 * chans, chans)
            turned = lax.dot_general(
                unit, block, (((1,), (1,)), ((), ())), preferred_element_type=F32).astype(BF16)
            for f in range(3):
                mat[f * chans : (f + 1) * chans, ae * chans : (ae + 1) * chans] = (
                    turned[:, f * chans : (f + 1) * chans])

    load1.wait()
    turn(raw1, mat1)
    load2.wait()
    turn(raw2, mat2)
    bias[0] = jnp.broadcast_to(b1[...], (depth, chans)).T
    bias[1] = jnp.broadcast_to(b2[...], (depth, chans)).T

    for h in range(2):
        relay(h)
        if h + 2 < len(chunks):
            begin(h + 2)

    lane = lax.broadcasted_iota(jnp.int32, (chans, depth), 1)

    def layer(source, mat, layer_bias, g, store):
        at = pl.multiple_of(g * group, group)
        stacked = jnp.concatenate(
            [source[a, :, pl.ds(pl.multiple_of(at + e * depth, depth), group)]
             for a in range(3) for e in range(3)], axis=0)
        products = jnp.dot(mat[...], stacked, preferred_element_type=F32)
        for r in range(PAIR):
            cols = slice(r * depth, (r + 1) * depth)
            left = pltpu.roll(products[0:chans, cols], 1, 1)
            right = pltpu.roll(products[2 * chans : 3 * chans, cols], depth - 1, 1)
            total = products[chans : 2 * chans, cols] + layer_bias
            total = total + jnp.where(lane == 0, 0.0, left)
            total = total + jnp.where(lane == depth - 1, 0.0, right)
            store(at + r * depth, jnp.maximum(total, 0.0).astype(BF16))

    def keep(at, value):
        hidden[1, :, pl.ds(pl.multiple_of(at + depth, depth), depth)] = value

    def finish(at, value):
        result[:, pl.ds(pl.multiple_of(at, depth), depth)] = value

    def to_h(d, g):
        space, plane = ways[d][3:]
        cols = pl.ds(pl.multiple_of(g * group + depth, depth), group)
        return pltpu.make_async_remote_copy(
            src_ref=hidden.at[1, :, cols], dst_ref=hidden.at[plane, :, cols],
            send_sem=h_send.at[d, g], recv_sem=h_recv.at[d, g],
            device_id=(space, c), device_id_type=MESH)

    always = s >= 0
    planes = ((0, has_hi, has_lo, s_up, 0), (1, has_lo, has_hi, s_dn, 2), (2, always, always, s, 1))
    rims = ((0, c_lo, c_hi, c_dn, depth, wide - depth), (1, c_hi, c_lo, c_up, width, 0))
    to_e = {(d, t): pltpu.make_async_remote_copy(
        src_ref=hidden.at[1, :, pl.ds(src_at, depth)],
        dst_ref=hidden.at[plane, :, pl.ds(dst_at, depth)],
        send_sem=e_send.at[d, t], recv_sem=e_recv.at[d, t],
        device_id=(space, chan), device_id_type=MESH)
        for d, _, _, space, plane in planes for t, _, _, chan, src_at, dst_at in rims}

    def send_edge(t):
        for d, sends, _, _, _ in planes:
            @pl.when(sends & rims[t][1])
            def _(d=d):
                to_e[d, t].start()

    def await_edge(t):
        for d, _, comes, _, _ in planes:
            @pl.when(comes & rims[t][2])
            def _(d=d):
                to_e[d, t].wait_recv()

    def await_x(h):
        local[h].wait()
        for d, _, comes, _, _ in ways:
            @pl.when(comes)
            def _(d=d):
                for k in range(nc):
                    to_x[d, k, h].wait_recv()

    def first_layer(step):
        g = lax.rem(step + groups - 1, groups)
        layer(field, mat1, bias[0], g, keep)

        @pl.when(step == 0)
        def _():
            send_edge(1)

        @pl.when(step == 1)
        def _():
            send_edge(0)

        for d, sends, _, _, _ in ways:
            @pl.when(sends)
            def _(d=d):
                to_h(d, g).start()

    @pl.loop(0, 2)
    def _(step):
        for h in range(2):
            @pl.when(step == h)
            def _(h=h):
                await_x(h)

        first_layer(step)

    for h in range(2, len(chunks)):
        relay(h)

    def await_h(g):
        for d, _, comes, _, _ in ways:
            @pl.when(comes)
            def _(d=d):
                to_h(d, g).wait_recv()

    def to_o(k, g):
        here = pl.ds(pl.multiple_of(g * group, group), group)
        there = pl.ds(pl.multiple_of(c * width + g * group, group), group)
        return pltpu.make_async_remote_copy(
            src_ref=result.at[part(peers[k]), here], dst_ref=out.at[:, there],
            send_sem=o_send.at[k - 1, g], recv_sem=o_recv.at[k - 1, g],
            device_id=(s, peers[k]), device_id_type=MESH)

    def own_o(g):
        here = pl.ds(pl.multiple_of(g * group, group), group)
        there = pl.ds(pl.multiple_of(c * width + g * group, group), group)
        return pltpu.make_async_copy(
            result.at[part(c), here], out.at[:, there], o_local.at[g])

    def second_layer(g):
        @pl.when(g == 0)
        def _():
            await_h(0)
            await_edge(1)

        @pl.when(g < groups - 1)
        def _():
            await_h(g + 1)

        @pl.when(g == groups - 1)
        def _():
            await_edge(0)

        layer(hidden, mat2, bias[1], g, finish)
        for k in range(1, nc):
            to_o(k, g).start()
        own_o(g).start()

    late = firsts[-1]
    if late > 2:
        @pl.loop(2, late)
        def _(step):
            for h, first in enumerate(firsts):
                if 2 <= h < len(chunks) - 1:
                    @pl.when(step == first)
                    def _(h=h):
                        await_x(h)

            first_layer(step)

    await_x(len(chunks) - 1)

    @pl.loop(late, groups)
    def _(step):
        first_layer(step)
        second_layer(step - late)

    @pl.loop(groups - late, groups)
    def _(g):
        second_layer(g)

    for (k, h), copy in to_z.items():
        copy.wait_send()
    for d, sends, _, _, _ in ways:
        @pl.when(sends)
        def _(d=d):
            for k in range(nc):
                for h in range(len(chunks)):
                    to_x[d, k, h].wait_send()

            @pl.loop(0, groups)
            def _(g):
                to_h(d, g).wait_send()
    for d, sends, _, _, _ in planes:
        for t, goes, _, _, _, _ in rims:
            @pl.when(sends & goes)
            def _(d=d, t=t):
                to_e[d, t].wait_send()

    @pl.loop(0, groups)
    def _(g):
        for k in range(1, nc):
            to_o(k, g).wait()
        own_o(g).wait()


def per_device(volume, weight_one, bias_one, weight_two, bias_two):
    own, planes, height, depth = volume.shape
    ns, nc = lax.axis_size("space"), lax.axis_size("chan")
    rows = height // nc
    chans = own * nc
    wide = (rows + 2) * depth
    cuts = len(row_chunks(rows))
    flat = jnp.pad(volume.reshape(own, height * depth), ((0, 0), (depth, depth)))
    dma = pltpu.SemaphoreType.DMA
    any_space = pl.BlockSpec(memory_space=pl.ANY)
    vmem = pl.BlockSpec(memory_space=pltpu.VMEM)
    macs = 27 * chans * chans * rows * depth
    result = pl.pallas_call(
        functools.partial(kernel, ns, nc, rows, depth, own),
        out_shape=jax.ShapeDtypeStruct((own, height * depth), BF16),
        in_specs=[any_space, any_space, vmem, any_space, vmem],
        out_specs=any_space,
        scratch_shapes=[
            pltpu.VMEM((3, chans, wide), BF16),
            pltpu.VMEM((3, chans, wide), BF16),
            pltpu.VMEM((chans, rows * depth), BF16),
            pltpu.VMEM(weight_one.shape, BF16),
            pltpu.VMEM(weight_two.shape, BF16),
            pltpu.VMEM((3 * chans, 9 * chans), BF16),
            pltpu.VMEM((3 * chans, 9 * chans), BF16),
            pltpu.VMEM((2, chans, depth), F32),
            dma((2,)), dma((cuts,)),
            dma((nc - 1, cuts)), dma((nc - 1, cuts)),
            dma((2, nc, cuts)), dma((2, nc, cuts)),
            dma((2, rows // PAIR)), dma((2, rows // PAIR)),
            dma((3, 2)), dma((3, 2)),
            dma((nc - 1, rows // PAIR)), dma((nc - 1, rows // PAIR)), dma((rows // PAIR,)),
        ],
        compiler_params=pltpu.CompilerParams(
            collective_id=0, has_side_effects=True, vmem_limit_bytes=40 * 2**20),
        cost_estimate=pl.CostEstimate(
            flops=4 * macs, bytes_accessed=4 * 2**20, transcendentals=0),
        name="conv_pair",
    )(flat, weight_one, bias_one.reshape(1, chans), weight_two, bias_two.reshape(1, chans))
    return result.reshape(own, planes, height, depth)


def solution(mesh):
    placed = (P("chan", "space", None, None), P(), P(), P(), P())
    return jax.shard_map(
        per_device,
        mesh=mesh,
        in_specs=placed,
        out_specs=P("chan", "space", None, None),
        check_vma=False,
    )
```

```python
import functools

import jax
import jax.numpy as jnp
from jax import lax
from jax.experimental import pallas as pl
from jax.experimental.pallas import tpu as pltpu
from jax.sharding import PartitionSpec as P

MESH = pl.DeviceIdType.MESH
BF16 = jnp.bfloat16
F32 = jnp.float32
PAIR = 2


def row_chunks(rows):
    chunks = [(rows - 2, 4), (0, 4)]
    start = 4
    while start < rows - 2:
        size = min(6, rows - 2 - start)
        chunks.append((start, size))
        start += size
    return chunks


def kernel(ns, nc, rows, depth, own, vol, w1, b1, w2, b2, out,
           field, hidden, result, raw1, raw2, mat1, mat2, bias,
           w_sem, local_sem, z_send, z_recv, x_send, x_recv,
           h_send, h_recv, e_send, e_recv, o_send, o_recv, o_local):
    s = lax.axis_index("space")
    c = lax.axis_index("chan")
    chans = own * nc
    has_lo, has_hi = s > 0, s < ns - 1
    c_lo, c_hi = c > 0, c < nc - 1
    s_dn, s_up = jnp.maximum(s - 1, 0), jnp.minimum(s + 1, ns - 1)
    c_dn, c_up = jnp.maximum(c - 1, 0), jnp.minimum(c + 1, nc - 1)
    peers = [lax.rem(c + k, nc) for k in range(nc)]
    sources = [lax.rem(c + nc - k, nc) for k in range(nc)]
    width = rows * depth
    wide = width + 2 * depth
    groups = rows // PAIR
    group = PAIR * depth
    chunks = row_chunks(rows)
    firsts = [0, 1] + [start // PAIR for start, _ in chunks[2:]]

    load1 = pltpu.make_async_copy(w1, raw1, w_sem.at[0])
    load2 = pltpu.make_async_copy(w2, raw2, w_sem.at[1])
    load1.start()
    load2.start()

    @pl.when(s == 0)
    def _():
        field[0] = jnp.zeros((chans, wide), BF16)
        hidden[0] = jnp.zeros((chans, wide), BF16)

    @pl.when(s == ns - 1)
    def _():
        field[2] = jnp.zeros((chans, wide), BF16)
        hidden[2] = jnp.zeros((chans, wide), BF16)

    @pl.when(c == 0)
    def _():
        hidden[:, :, 0:depth] = jnp.zeros((3, chans, depth), BF16)

    @pl.when(c == nc - 1)
    def _():
        hidden[:, :, wide - depth : wide] = jnp.zeros((3, chans, depth), BF16)

    barrier = pltpu.get_barrier_semaphore()

    def greet(space, chan):
        pl.semaphore_signal(barrier, inc=1, device_id=(space, chan), device_id_type=MESH)

    for k in range(1, nc):
        greet(s, peers[k])
    for there, space in ((has_lo, s_dn), (has_hi, s_up)):
        @pl.when(there)
        def _(space=space):
            greet(space, c)

        @pl.when(there & c_lo)
        def _(space=space):
            greet(space, c_dn)

        @pl.when(there & c_hi)
        def _(space=space):
            greet(space, c_up)
    sides = has_lo.astype(jnp.int32) + has_hi.astype(jnp.int32)
    edges = c_lo.astype(jnp.int32) + c_hi.astype(jnp.int32)
    pl.semaphore_wait(barrier, nc - 1 + sides * (1 + edges))

    def part(index):
        return pl.ds(pl.multiple_of(index * own, own), own)

    def window(index, h):
        start, size = chunks[h]
        return pl.ds(pl.multiple_of(index * width + start * depth, depth), size * depth)

    def landed(h):
        start, size = chunks[h]
        return pl.ds(start * depth, size * depth)

    local = [pltpu.make_async_copy(
        vol.at[:, window(c, h)], field.at[1, part(c), landed(h)], local_sem.at[h])
        for h in range(len(chunks))]
    to_z = {(k, h): pltpu.make_async_remote_copy(
        src_ref=vol.at[:, window(peers[k], h)],
        dst_ref=field.at[1, part(c), landed(h)],
        send_sem=z_send.at[k - 1, h], recv_sem=z_recv.at[k - 1, h],
        device_id=(s, peers[k]), device_id_type=MESH)
        for h in range(len(chunks)) for k in range(1, nc)}
    ways = ((0, has_hi, has_lo, s_up, 0), (1, has_lo, has_hi, s_dn, 2))
    to_x = {}
    for d, _, _, space, plane in ways:
        for h in range(len(chunks)):
            for k in range(nc):
                if k == 0:
                    src = vol.at[:, window(c, h)]
                else:
                    src = field.at[1, part(sources[k]), landed(h)]
                to_x[d, k, h] = pltpu.make_async_remote_copy(
                    src_ref=src,
                    dst_ref=field.at[plane, part(sources[k]), landed(h)],
                    send_sem=x_send.at[d, k, h], recv_sem=x_recv.at[d, k, h],
                    device_id=(space, c), device_id_type=MESH)

    def forward(k, h):
        for d, sends, _, _, _ in ways:
            @pl.when(sends)
            def _(d=d):
                to_x[d, k, h].start()

    def begin(h):
        for k in range(1, nc):
            to_z[k, h].start()
        local[h].start()
        forward(0, h)

    def relay(h):
        for k in range(1, nc):
            to_z[k, h].wait_recv()
            forward(k, h)

    begin(0)

    unit = jnp.where(
        lax.broadcasted_iota(jnp.int32, (chans, chans), 0)
        == lax.broadcasted_iota(jnp.int32, (chans, chans), 1), 1.0, 0.0).astype(BF16)

    def turn(raw, mat):
        for ae in range(9):
            block = raw[3 * ae : 3 * ae + 3].reshape(3 * chans, chans)
            turned = lax.dot_general(
                unit, block, (((1,), (1,)), ((), ())), preferred_element_type=F32).astype(BF16)
            for f in range(3):
                mat[f * chans : (f + 1) * chans, ae * chans : (ae + 1) * chans] = (
                    turned[:, f * chans : (f + 1) * chans])

    load1.wait()
    turn(raw1, mat1)
    begin(1)
    load2.wait()
    turn(raw2, mat2)
    bias[0] = jnp.broadcast_to(b1[...], (depth, chans)).T
    bias[1] = jnp.broadcast_to(b2[...], (depth, chans)).T

    for h in range(2):
        relay(h)
        if h + 2 < len(chunks):
            begin(h + 2)

    lane = lax.broadcasted_iota(jnp.int32, (chans, depth), 1)

    def layer(source, mat, layer_bias, g, store):
        at = pl.multiple_of(g * group, group)
        stacked = jnp.concatenate(
            [source[a, :, pl.ds(pl.multiple_of(at + e * depth, depth), group)]
             for a in range(3) for e in range(3)], axis=0)
        products = jnp.dot(mat[...], stacked, preferred_element_type=F32)
        for r in range(PAIR):
            cols = slice(r * depth, (r + 1) * depth)
            left = pltpu.roll(products[0:chans, cols], 1, 1)
            right = pltpu.roll(products[2 * chans : 3 * chans, cols], depth - 1, 1)
            total = products[chans : 2 * chans, cols] + layer_bias
            total = total + jnp.where(lane == 0, 0.0, left)
            total = total + jnp.where(lane == depth - 1, 0.0, right)
            store(at + r * depth, jnp.maximum(total, 0.0).astype(BF16))

    def keep(at, value):
        hidden[1, :, pl.ds(pl.multiple_of(at + depth, depth), depth)] = value

    def finish(at, value):
        result[:, pl.ds(pl.multiple_of(at, depth), depth)] = value

    def to_h(d, g):
        space, plane = ways[d][3:]
        cols = pl.ds(pl.multiple_of(g * group + depth, depth), group)
        return pltpu.make_async_remote_copy(
            src_ref=hidden.at[1, :, cols], dst_ref=hidden.at[plane, :, cols],
            send_sem=h_send.at[d, g], recv_sem=h_recv.at[d, g],
            device_id=(space, c), device_id_type=MESH)

    always = s >= 0
    planes = ((0, has_hi, has_lo, s_up, 0), (1, has_lo, has_hi, s_dn, 2), (2, always, always, s, 1))
    rims = ((0, c_lo, c_hi, c_dn, depth, wide - depth), (1, c_hi, c_lo, c_up, width, 0))
    to_e = {(d, t): pltpu.make_async_remote_copy(
        src_ref=hidden.at[1, :, pl.ds(src_at, depth)],
        dst_ref=hidden.at[plane, :, pl.ds(dst_at, depth)],
        send_sem=e_send.at[d, t], recv_sem=e_recv.at[d, t],
        device_id=(space, chan), device_id_type=MESH)
        for d, _, _, space, plane in planes for t, _, _, chan, src_at, dst_at in rims}

    def send_edge(t):
        for d, sends, _, _, _ in planes:
            @pl.when(sends & rims[t][1])
            def _(d=d):
                to_e[d, t].start()

    def await_edge(t):
        for d, _, comes, _, _ in planes:
            @pl.when(comes & rims[t][2])
            def _(d=d):
                to_e[d, t].wait_recv()

    def await_x(h):
        local[h].wait()
        for d, _, comes, _, _ in ways:
            @pl.when(comes)
            def _(d=d):
                for k in range(nc):
                    to_x[d, k, h].wait_recv()

    def first_layer(step):
        g = lax.rem(step + groups - 1, groups)
        layer(field, mat1, bias[0], g, keep)

        @pl.when(step == 0)
        def _():
            send_edge(1)

        @pl.when(step == 1)
        def _():
            send_edge(0)

        for d, sends, _, _, _ in ways:
            @pl.when(sends)
            def _(d=d):
                to_h(d, g).start()

    @pl.loop(0, 2)
    def _(step):
        for h in range(2):
            @pl.when(step == h)
            def _(h=h):
                await_x(h)

        first_layer(step)

    for h in range(2, len(chunks)):
        relay(h)

    @pl.loop(2, groups)
    def _(step):
        for h, first in enumerate(firsts):
            if h >= 2:
                @pl.when(step == first)
                def _(h=h):
                    await_x(h)

        first_layer(step)

    def await_h(g):
        for d, _, comes, _, _ in ways:
            @pl.when(comes)
            def _(d=d):
                to_h(d, g).wait_recv()

    def to_o(k, g):
        here = pl.ds(pl.multiple_of(g * group, group), group)
        there = pl.ds(pl.multiple_of(c * width + g * group, group), group)
        return pltpu.make_async_remote_copy(
            src_ref=result.at[part(peers[k]), here], dst_ref=out.at[:, there],
            send_sem=o_send.at[k - 1, g], recv_sem=o_recv.at[k - 1, g],
            device_id=(s, peers[k]), device_id_type=MESH)

    def own_o(g):
        here = pl.ds(pl.multiple_of(g * group, group), group)
        there = pl.ds(pl.multiple_of(c * width + g * group, group), group)
        return pltpu.make_async_copy(
            result.at[part(c), here], out.at[:, there], o_local.at[g])

    await_h(0)
    await_edge(1)

    @pl.loop(0, groups)
    def _(g):
        @pl.when(g < groups - 1)
        def _():
            await_h(g + 1)

        @pl.when(g == groups - 1)
        def _():
            await_edge(0)

        layer(hidden, mat2, bias[1], g, finish)
        for k in range(1, nc):
            to_o(k, g).start()
        own_o(g).start()

    for (k, h), copy in to_z.items():
        copy.wait_send()
    for d, sends, _, _, _ in ways:
        @pl.when(sends)
        def _(d=d):
            for k in range(nc):
                for h in range(len(chunks)):
                    to_x[d, k, h].wait_send()

            @pl.loop(0, groups)
            def _(g):
                to_h(d, g).wait_send()
    for d, sends, _, _, _ in planes:
        for t, goes, _, _, _, _ in rims:
            @pl.when(sends & goes)
            def _(d=d, t=t):
                to_e[d, t].wait_send()

    @pl.loop(0, groups)
    def _(g):
        for k in range(1, nc):
            to_o(k, g).wait()
        own_o(g).wait()


def per_device(volume, weight_one, bias_one, weight_two, bias_two):
    own, planes, height, depth = volume.shape
    ns, nc = lax.axis_size("space"), lax.axis_size("chan")
    rows = height // nc
    chans = own * nc
    wide = (rows + 2) * depth
    cuts = len(row_chunks(rows))
    flat = jnp.pad(volume.reshape(own, height * depth), ((0, 0), (depth, depth)))
    dma = pltpu.SemaphoreType.DMA
    any_space = pl.BlockSpec(memory_space=pl.ANY)
    vmem = pl.BlockSpec(memory_space=pltpu.VMEM)
    macs = 27 * chans * chans * rows * depth
    result = pl.pallas_call(
        functools.partial(kernel, ns, nc, rows, depth, own),
        out_shape=jax.ShapeDtypeStruct((own, height * depth), BF16),
        in_specs=[any_space, any_space, vmem, any_space, vmem],
        out_specs=any_space,
        scratch_shapes=[
            pltpu.VMEM((3, chans, wide), BF16),
            pltpu.VMEM((3, chans, wide), BF16),
            pltpu.VMEM((chans, rows * depth), BF16),
            pltpu.VMEM(weight_one.shape, BF16),
            pltpu.VMEM(weight_two.shape, BF16),
            pltpu.VMEM((3 * chans, 9 * chans), BF16),
            pltpu.VMEM((3 * chans, 9 * chans), BF16),
            pltpu.VMEM((2, chans, depth), F32),
            dma((2,)), dma((cuts,)),
            dma((nc - 1, cuts)), dma((nc - 1, cuts)),
            dma((2, nc, cuts)), dma((2, nc, cuts)),
            dma((2, rows // PAIR)), dma((2, rows // PAIR)),
            dma((3, 2)), dma((3, 2)),
            dma((nc - 1, rows // PAIR)), dma((nc - 1, rows // PAIR)), dma((rows // PAIR,)),
        ],
        compiler_params=pltpu.CompilerParams(
            collective_id=0, has_side_effects=True, vmem_limit_bytes=40 * 2**20),
        cost_estimate=pl.CostEstimate(
            flops=4 * macs, bytes_accessed=4 * 2**20, transcendentals=0),
        name="conv_pair",
    )(flat, weight_one, bias_one.reshape(1, chans), weight_two, bias_two.reshape(1, chans))
    return result.reshape(own, planes, height, depth)


def solution(mesh):
    placed = (P("chan", "space", None, None), P(), P(), P(), P())
    return jax.shard_map(
        per_device,
        mesh=mesh,
        in_specs=placed,
        out_specs=P("chan", "space", None, None),
        check_vma=False,
    )
```

```python
import functools

import jax
import jax.numpy as jnp
from jax import lax
from jax.experimental import pallas as pl
from jax.experimental.pallas import tpu as pltpu
from jax.sharding import PartitionSpec as P

MESH = pl.DeviceIdType.MESH
BF16 = jnp.bfloat16
F32 = jnp.float32
PAIR = 2


def row_chunks(rows):
    chunks = [(rows - 2, 4), (0, 4)]
    start = 4
    while start < rows - 2:
        size = min(6, rows - 2 - start)
        chunks.append((start, size))
        start += size
    return chunks


def kernel(ns, nc, rows, depth, own, vol, w1, b1, w2, b2, out,
           field, hidden, result, raw1, raw2, mat1, mat2, bias,
           w_sem, local_sem, z_send, z_recv, x_send, x_recv,
           h_send, h_recv, e_send, e_recv, o_send, o_recv, o_local):
    s = lax.axis_index("space")
    c = lax.axis_index("chan")
    chans = own * nc
    has_lo, has_hi = s > 0, s < ns - 1
    c_lo, c_hi = c > 0, c < nc - 1
    s_dn, s_up = jnp.maximum(s - 1, 0), jnp.minimum(s + 1, ns - 1)
    c_dn, c_up = jnp.maximum(c - 1, 0), jnp.minimum(c + 1, nc - 1)
    peers = [lax.rem(c + k, nc) for k in range(nc)]
    sources = [lax.rem(c + nc - k, nc) for k in range(nc)]
    width = rows * depth
    wide = width + 2 * depth
    groups = rows // PAIR
    group = PAIR * depth
    chunks = row_chunks(rows)
    firsts = [0, 1] + [start // PAIR for start, _ in chunks[2:]]

    load1 = pltpu.make_async_copy(w1, raw1, w_sem.at[0])
    load2 = pltpu.make_async_copy(w2, raw2, w_sem.at[1])
    load1.start()
    load2.start()

    @pl.when(s == 0)
    def _():
        field[0] = jnp.zeros((chans, wide), BF16)
        hidden[0] = jnp.zeros((chans, wide), BF16)

    @pl.when(s == ns - 1)
    def _():
        field[2] = jnp.zeros((chans, wide), BF16)
        hidden[2] = jnp.zeros((chans, wide), BF16)

    @pl.when(c == 0)
    def _():
        hidden[:, :, 0:depth] = jnp.zeros((3, chans, depth), BF16)

    @pl.when(c == nc - 1)
    def _():
        hidden[:, :, wide - depth : wide] = jnp.zeros((3, chans, depth), BF16)

    barrier = pltpu.get_barrier_semaphore()

    def greet(space, chan):
        pl.semaphore_signal(barrier, inc=1, device_id=(space, chan), device_id_type=MESH)

    for k in range(1, nc):
        greet(s, peers[k])
    for there, space in ((has_lo, s_dn), (has_hi, s_up)):
        @pl.when(there)
        def _(space=space):
            greet(space, c)

        @pl.when(there & c_lo)
        def _(space=space):
            greet(space, c_dn)

        @pl.when(there & c_hi)
        def _(space=space):
            greet(space, c_up)
    sides = has_lo.astype(jnp.int32) + has_hi.astype(jnp.int32)
    edges = c_lo.astype(jnp.int32) + c_hi.astype(jnp.int32)
    pl.semaphore_wait(barrier, nc - 1 + sides * (1 + edges))

    def part(index):
        return pl.ds(pl.multiple_of(index * own, own), own)

    def window(index, h):
        start, size = chunks[h]
        return pl.ds(pl.multiple_of(index * width + start * depth, depth), size * depth)

    def landed(h):
        start, size = chunks[h]
        return pl.ds(start * depth, size * depth)

    local = [pltpu.make_async_copy(
        vol.at[:, window(c, h)], field.at[1, part(c), landed(h)], local_sem.at[h])
        for h in range(len(chunks))]
    to_z = {(k, h): pltpu.make_async_remote_copy(
        src_ref=vol.at[:, window(peers[k], h)],
        dst_ref=field.at[1, part(c), landed(h)],
        send_sem=z_send.at[k - 1, h], recv_sem=z_recv.at[k - 1, h],
        device_id=(s, peers[k]), device_id_type=MESH)
        for h in range(len(chunks)) for k in range(1, nc)}
    ways = ((0, has_hi, has_lo, s_up, 0), (1, has_lo, has_hi, s_dn, 2))
    to_x = {}
    for d, _, _, space, plane in ways:
        for h in range(len(chunks)):
            for k in range(nc):
                if k == 0:
                    src = vol.at[:, window(c, h)]
                else:
                    src = field.at[1, part(sources[k]), landed(h)]
                to_x[d, k, h] = pltpu.make_async_remote_copy(
                    src_ref=src,
                    dst_ref=field.at[plane, part(sources[k]), landed(h)],
                    send_sem=x_send.at[d, k, h], recv_sem=x_recv.at[d, k, h],
                    device_id=(space, c), device_id_type=MESH)

    def forward(k, h):
        for d, sends, _, _, _ in ways:
            @pl.when(sends)
            def _(d=d):
                to_x[d, k, h].start()

    def begin(h):
        for k in range(1, nc):
            to_z[k, h].start()
        local[h].start()
        forward(0, h)

    def relay(h):
        for k in range(1, nc):
            to_z[k, h].wait_recv()
            forward(k, h)

    begin(0)
    begin(1)

    unit = jnp.where(
        lax.broadcasted_iota(jnp.int32, (chans, chans), 0)
        == lax.broadcasted_iota(jnp.int32, (chans, chans), 1), 1.0, 0.0).astype(BF16)

    def turn(raw, mat):
        for ae in range(9):
            block = raw[3 * ae : 3 * ae + 3].reshape(3 * chans, chans)
            turned = lax.dot_general(
                unit, block, (((1,), (1,)), ((), ())), preferred_element_type=F32).astype(BF16)
            for f in range(3):
                mat[f * chans : (f + 1) * chans, ae * chans : (ae + 1) * chans] = (
                    turned[:, f * chans : (f + 1) * chans])

    load1.wait()
    turn(raw1, mat1)
    load2.wait()
    turn(raw2, mat2)
    bias[0] = jnp.broadcast_to(b1[...], (depth, chans)).T
    bias[1] = jnp.broadcast_to(b2[...], (depth, chans)).T

    for h in range(2):
        relay(h)
        if h == 0 and len(chunks) > 2:
            begin(2)

    lane = lax.broadcasted_iota(jnp.int32, (chans, depth), 1)

    def layer(source, mat, layer_bias, g, store):
        at = pl.multiple_of(g * group, group)
        stacked = jnp.concatenate(
            [source[a, :, pl.ds(pl.multiple_of(at + e * depth, depth), group)]
             for a in range(3) for e in range(3)], axis=0)
        products = jnp.dot(mat[...], stacked, preferred_element_type=F32)
        for r in range(PAIR):
            cols = slice(r * depth, (r + 1) * depth)
            left = pltpu.roll(products[0:chans, cols], 1, 1)
            right = pltpu.roll(products[2 * chans : 3 * chans, cols], depth - 1, 1)
            total = products[chans : 2 * chans, cols] + layer_bias
            total = total + jnp.where(lane == 0, 0.0, left)
            total = total + jnp.where(lane == depth - 1, 0.0, right)
            store(at + r * depth, jnp.maximum(total, 0.0).astype(BF16))

    def keep(at, value):
        hidden[1, :, pl.ds(pl.multiple_of(at + depth, depth), depth)] = value

    def finish(at, value):
        result[:, pl.ds(pl.multiple_of(at, depth), depth)] = value

    def to_h(d, g):
        space, plane = ways[d][3:]
        cols = pl.ds(pl.multiple_of(g * group + depth, depth), group)
        return pltpu.make_async_remote_copy(
            src_ref=hidden.at[1, :, cols], dst_ref=hidden.at[plane, :, cols],
            send_sem=h_send.at[d, g], recv_sem=h_recv.at[d, g],
            device_id=(space, c), device_id_type=MESH)

    always = s >= 0
    planes = ((0, has_hi, has_lo, s_up, 0), (1, has_lo, has_hi, s_dn, 2), (2, always, always, s, 1))
    rims = ((0, c_lo, c_hi, c_dn, depth, wide - depth), (1, c_hi, c_lo, c_up, width, 0))
    to_e = {(d, t): pltpu.make_async_remote_copy(
        src_ref=hidden.at[1, :, pl.ds(src_at, depth)],
        dst_ref=hidden.at[plane, :, pl.ds(dst_at, depth)],
        send_sem=e_send.at[d, t], recv_sem=e_recv.at[d, t],
        device_id=(space, chan), device_id_type=MESH)
        for d, _, _, space, plane in planes for t, _, _, chan, src_at, dst_at in rims}

    def send_edge(t):
        for d, sends, _, _, _ in planes:
            @pl.when(sends & rims[t][1])
            def _(d=d):
                to_e[d, t].start()

    def await_edge(t):
        for d, _, comes, _, _ in planes:
            @pl.when(comes & rims[t][2])
            def _(d=d):
                to_e[d, t].wait_recv()

    def await_x(h):
        local[h].wait()
        for d, _, comes, _, _ in ways:
            @pl.when(comes)
            def _(d=d):
                for k in range(nc):
                    to_x[d, k, h].wait_recv()

    def first_layer(step):
        g = lax.rem(step + groups - 1, groups)
        layer(field, mat1, bias[0], g, keep)

        @pl.when(step == 0)
        def _():
            send_edge(1)

        @pl.when(step == 1)
        def _():
            send_edge(0)

        for d, sends, _, _, _ in ways:
            @pl.when(sends)
            def _(d=d):
                to_h(d, g).start()

    @pl.loop(0, 2)
    def _(step):
        for h in range(2):
            @pl.when(step == h)
            def _(h=h):
                await_x(h)
                if h == 0:
                    for later in range(3, len(chunks)):
                        begin(later)

        first_layer(step)

    if len(chunks) > 2:
        relay(2)

    @pl.loop(2, groups)
    def _(step):
        for h, first in enumerate(firsts):
            if h >= 2:
                @pl.when(step == first)
                def _(h=h):
                    if h > 2:
                        relay(h)
                    await_x(h)

        first_layer(step)

    def await_h(g):
        for d, _, comes, _, _ in ways:
            @pl.when(comes)
            def _(d=d):
                to_h(d, g).wait_recv()

    def to_o(k, g):
        here = pl.ds(pl.multiple_of(g * group, group), group)
        there = pl.ds(pl.multiple_of(c * width + g * group, group), group)
        return pltpu.make_async_remote_copy(
            src_ref=result.at[part(peers[k]), here], dst_ref=out.at[:, there],
            send_sem=o_send.at[k - 1, g], recv_sem=o_recv.at[k - 1, g],
            device_id=(s, peers[k]), device_id_type=MESH)

    def own_o(g):
        here = pl.ds(pl.multiple_of(g * group, group), group)
        there = pl.ds(pl.multiple_of(c * width + g * group, group), group)
        return pltpu.make_async_copy(
            result.at[part(c), here], out.at[:, there], o_local.at[g])

    await_h(0)
    await_edge(1)

    @pl.loop(0, groups)
    def _(g):
        @pl.when(g < groups - 1)
        def _():
            await_h(g + 1)

        @pl.when(g == groups - 1)
        def _():
            await_edge(0)

        layer(hidden, mat2, bias[1], g, finish)
        for k in range(1, nc):
            to_o(k, g).start()
        own_o(g).start()

    for (k, h), copy in to_z.items():
        copy.wait_send()
    for d, sends, _, _, _ in ways:
        @pl.when(sends)
        def _(d=d):
            for k in range(nc):
                for h in range(len(chunks)):
                    to_x[d, k, h].wait_send()

            @pl.loop(0, groups)
            def _(g):
                to_h(d, g).wait_send()
    for d, sends, _, _, _ in planes:
        for t, goes, _, _, _, _ in rims:
            @pl.when(sends & goes)
            def _(d=d, t=t):
                to_e[d, t].wait_send()

    @pl.loop(0, groups)
    def _(g):
        for k in range(1, nc):
            to_o(k, g).wait()
        own_o(g).wait()


def per_device(volume, weight_one, bias_one, weight_two, bias_two):
    own, planes, height, depth = volume.shape
    ns, nc = lax.axis_size("space"), lax.axis_size("chan")
    rows = height // nc
    chans = own * nc
    wide = (rows + 2) * depth
    cuts = len(row_chunks(rows))
    flat = jnp.pad(volume.reshape(own, height * depth), ((0, 0), (depth, depth)))
    dma = pltpu.SemaphoreType.DMA
    any_space = pl.BlockSpec(memory_space=pl.ANY)
    vmem = pl.BlockSpec(memory_space=pltpu.VMEM)
    macs = 27 * chans * chans * rows * depth
    result = pl.pallas_call(
        functools.partial(kernel, ns, nc, rows, depth, own),
        out_shape=jax.ShapeDtypeStruct((own, height * depth), BF16),
        in_specs=[any_space, any_space, vmem, any_space, vmem],
        out_specs=any_space,
        scratch_shapes=[
            pltpu.VMEM((3, chans, wide), BF16),
            pltpu.VMEM((3, chans, wide), BF16),
            pltpu.VMEM((chans, rows * depth), BF16),
            pltpu.VMEM(weight_one.shape, BF16),
            pltpu.VMEM(weight_two.shape, BF16),
            pltpu.VMEM((3 * chans, 9 * chans), BF16),
            pltpu.VMEM((3 * chans, 9 * chans), BF16),
            pltpu.VMEM((2, chans, depth), F32),
            dma((2,)), dma((cuts,)),
            dma((nc - 1, cuts)), dma((nc - 1, cuts)),
            dma((2, nc, cuts)), dma((2, nc, cuts)),
            dma((2, rows // PAIR)), dma((2, rows // PAIR)),
            dma((3, 2)), dma((3, 2)),
            dma((nc - 1, rows // PAIR)), dma((nc - 1, rows // PAIR)), dma((rows // PAIR,)),
        ],
        compiler_params=pltpu.CompilerParams(
            collective_id=0, has_side_effects=True, vmem_limit_bytes=40 * 2**20),
        cost_estimate=pl.CostEstimate(
            flops=4 * macs, bytes_accessed=4 * 2**20, transcendentals=0),
        name="conv_pair",
    )(flat, weight_one, bias_one.reshape(1, chans), weight_two, bias_two.reshape(1, chans))
    return result.reshape(own, planes, height, depth)


def solution(mesh):
    placed = (P("chan", "space", None, None), P(), P(), P(), P())
    return jax.shard_map(
        per_device,
        mesh=mesh,
        in_specs=placed,
        out_specs=P("chan", "space", None, None),
        check_vma=False,
    )
```

```python
import functools

import jax
import jax.numpy as jnp
from jax import lax
from jax.experimental import pallas as pl
from jax.experimental.pallas import tpu as pltpu
from jax.sharding import PartitionSpec as P

MESH = pl.DeviceIdType.MESH
BF16 = jnp.bfloat16
F32 = jnp.float32
PAIR = 2


def row_chunks(rows):
    chunks = [(rows - 2, 4), (0, 4)]
    start = 4
    while start < rows - 2:
        size = min(6, rows - 2 - start)
        chunks.append((start, size))
        start += size
    return chunks


def kernel(ns, nc, rows, depth, own, vol, w1, b1, w2, b2, out,
           field, hidden, result, raw1, raw2, mat1, mat2, bias, raw_bias,
           w_sem, local_sem, z_send, z_recv, x_send, x_recv,
           h_send, h_recv, e_send, e_recv, o_send, o_recv, o_local):
    s = lax.axis_index("space")
    c = lax.axis_index("chan")
    chans = own * nc
    has_lo, has_hi = s > 0, s < ns - 1
    c_lo, c_hi = c > 0, c < nc - 1
    s_dn, s_up = jnp.maximum(s - 1, 0), jnp.minimum(s + 1, ns - 1)
    c_dn, c_up = jnp.maximum(c - 1, 0), jnp.minimum(c + 1, nc - 1)
    peers = [lax.rem(c + k, nc) for k in range(nc)]
    sources = [lax.rem(c + nc - k, nc) for k in range(nc)]
    width = rows * depth
    wide = width + 2 * depth
    groups = rows // PAIR
    group = PAIR * depth
    chunks = row_chunks(rows)
    firsts = [0, 1] + [start // PAIR for start, _ in chunks[2:]]

    load1 = pltpu.make_async_copy(w1, raw1, w_sem.at[0])
    load2 = pltpu.make_async_copy(w2, raw2, w_sem.at[1])
    load3 = pltpu.make_async_copy(b1, raw_bias.at[0], w_sem.at[2])
    load4 = pltpu.make_async_copy(b2, raw_bias.at[1], w_sem.at[3])
    load1.start()
    load2.start()
    load3.start()
    load4.start()

    @pl.when(s == 0)
    def _():
        field[0] = jnp.zeros((chans, wide), BF16)
        hidden[0] = jnp.zeros((chans, wide), BF16)

    @pl.when(s == ns - 1)
    def _():
        field[2] = jnp.zeros((chans, wide), BF16)
        hidden[2] = jnp.zeros((chans, wide), BF16)

    @pl.when(c == 0)
    def _():
        hidden[:, :, 0:depth] = jnp.zeros((3, chans, depth), BF16)

    @pl.when(c == nc - 1)
    def _():
        hidden[:, :, wide - depth : wide] = jnp.zeros((3, chans, depth), BF16)

    barrier = pltpu.get_barrier_semaphore()

    def greet(space, chan):
        pl.semaphore_signal(barrier, inc=1, device_id=(space, chan), device_id_type=MESH)

    for k in range(1, nc):
        greet(s, peers[k])
    for there, space in ((has_lo, s_dn), (has_hi, s_up)):
        @pl.when(there)
        def _(space=space):
            greet(space, c)

        @pl.when(there & c_lo)
        def _(space=space):
            greet(space, c_dn)

        @pl.when(there & c_hi)
        def _(space=space):
            greet(space, c_up)
    sides = has_lo.astype(jnp.int32) + has_hi.astype(jnp.int32)
    edges = c_lo.astype(jnp.int32) + c_hi.astype(jnp.int32)
    pl.semaphore_wait(barrier, nc - 1 + sides * (1 + edges))

    def part(index):
        return pl.ds(pl.multiple_of(index * own, own), own)

    def window(index, h):
        start, size = chunks[h]
        return pl.ds(pl.multiple_of(index * width + start * depth, depth), size * depth)

    def landed(h):
        start, size = chunks[h]
        return pl.ds(start * depth, size * depth)

    local = [pltpu.make_async_copy(
        vol.at[:, window(c, h)], field.at[1, part(c), landed(h)], local_sem.at[h])
        for h in range(len(chunks))]
    to_z = {(k, h): pltpu.make_async_remote_copy(
        src_ref=vol.at[:, window(peers[k], h)],
        dst_ref=field.at[1, part(c), landed(h)],
        send_sem=z_send.at[k - 1, h], recv_sem=z_recv.at[k - 1, h],
        device_id=(s, peers[k]), device_id_type=MESH)
        for h in range(len(chunks)) for k in range(1, nc)}
    ways = ((0, has_hi, has_lo, s_up, 0), (1, has_lo, has_hi, s_dn, 2))
    to_x = {}
    for d, _, _, space, plane in ways:
        for h in range(len(chunks)):
            for k in range(nc):
                if k == 0:
                    src = vol.at[:, window(c, h)]
                else:
                    src = field.at[1, part(sources[k]), landed(h)]
                to_x[d, k, h] = pltpu.make_async_remote_copy(
                    src_ref=src,
                    dst_ref=field.at[plane, part(sources[k]), landed(h)],
                    send_sem=x_send.at[d, k, h], recv_sem=x_recv.at[d, k, h],
                    device_id=(space, c), device_id_type=MESH)

    def forward(k, h):
        for d, sends, _, _, _ in ways:
            @pl.when(sends)
            def _(d=d):
                to_x[d, k, h].start()

    def begin(h):
        for k in range(1, nc):
            to_z[k, h].start()
        local[h].start()
        forward(0, h)

    def relay(h):
        for k in range(1, nc):
            to_z[k, h].wait_recv()
            forward(k, h)

    begin(0)
    begin(1)

    unit = jnp.where(
        lax.broadcasted_iota(jnp.int32, (chans, chans), 0)
        == lax.broadcasted_iota(jnp.int32, (chans, chans), 1), 1.0, 0.0).astype(BF16)

    def turn(raw, mat):
        for ae in range(9):
            block = raw[3 * ae : 3 * ae + 3].reshape(3 * chans, chans)
            turned = lax.dot_general(
                unit, block, (((1,), (1,)), ((), ())), preferred_element_type=F32).astype(BF16)
            for f in range(3):
                mat[f * chans : (f + 1) * chans, ae * chans : (ae + 1) * chans] = (
                    turned[:, f * chans : (f + 1) * chans])

    load1.wait()
    turn(raw1, mat1)
    load2.wait()
    turn(raw2, mat2)
    load3.wait()
    load4.wait()
    bias[0] = jnp.broadcast_to(raw_bias[0], (depth, chans)).T
    bias[1] = jnp.broadcast_to(raw_bias[1], (depth, chans)).T

    for h in range(2):
        relay(h)
        if h + 2 < len(chunks):
            begin(h + 2)

    lane = lax.broadcasted_iota(jnp.int32, (chans, depth), 1)

    def layer(source, mat, layer_bias, g, store):
        at = pl.multiple_of(g * group, group)
        stacked = jnp.concatenate(
            [source[a, :, pl.ds(pl.multiple_of(at + e * depth, depth), group)]
             for a in range(3) for e in range(3)], axis=0)
        products = jnp.dot(mat[...], stacked, preferred_element_type=F32)
        for r in range(PAIR):
            cols = slice(r * depth, (r + 1) * depth)
            left = pltpu.roll(products[0:chans, cols], 1, 1)
            right = pltpu.roll(products[2 * chans : 3 * chans, cols], depth - 1, 1)
            total = products[chans : 2 * chans, cols] + layer_bias
            total = total + jnp.where(lane == 0, 0.0, left)
            total = total + jnp.where(lane == depth - 1, 0.0, right)
            store(at + r * depth, jnp.maximum(total, 0.0).astype(BF16))

    def keep(at, value):
        hidden[1, :, pl.ds(pl.multiple_of(at + depth, depth), depth)] = value

    def finish(at, value):
        result[:, pl.ds(pl.multiple_of(at, depth), depth)] = value

    def to_h(d, g):
        space, plane = ways[d][3:]
        cols = pl.ds(pl.multiple_of(g * group + depth, depth), group)
        return pltpu.make_async_remote_copy(
            src_ref=hidden.at[1, :, cols], dst_ref=hidden.at[plane, :, cols],
            send_sem=h_send.at[d, g], recv_sem=h_recv.at[d, g],
            device_id=(space, c), device_id_type=MESH)

    always = s >= 0
    planes = ((0, has_hi, has_lo, s_up, 0), (1, has_lo, has_hi, s_dn, 2), (2, always, always, s, 1))
    rims = ((0, c_lo, c_hi, c_dn, depth, wide - depth), (1, c_hi, c_lo, c_up, width, 0))
    to_e = {(d, t): pltpu.make_async_remote_copy(
        src_ref=hidden.at[1, :, pl.ds(src_at, depth)],
        dst_ref=hidden.at[plane, :, pl.ds(dst_at, depth)],
        send_sem=e_send.at[d, t], recv_sem=e_recv.at[d, t],
        device_id=(space, chan), device_id_type=MESH)
        for d, _, _, space, plane in planes for t, _, _, chan, src_at, dst_at in rims}

    def send_edge(t):
        for d, sends, _, _, _ in planes:
            @pl.when(sends & rims[t][1])
            def _(d=d):
                to_e[d, t].start()

    def await_edge(t):
        for d, _, comes, _, _ in planes:
            @pl.when(comes & rims[t][2])
            def _(d=d):
                to_e[d, t].wait_recv()

    def await_x(h):
        local[h].wait()
        for d, _, comes, _, _ in ways:
            @pl.when(comes)
            def _(d=d):
                for k in range(nc):
                    to_x[d, k, h].wait_recv()

    def first_layer(step):
        g = lax.rem(step + groups - 1, groups)
        layer(field, mat1, bias[0], g, keep)

        @pl.when(step == 0)
        def _():
            send_edge(1)

        @pl.when(step == 1)
        def _():
            send_edge(0)

        for d, sends, _, _, _ in ways:
            @pl.when(sends)
            def _(d=d):
                to_h(d, g).start()

    @pl.loop(0, 2)
    def _(step):
        for h in range(2):
            @pl.when(step == h)
            def _(h=h):
                await_x(h)

        first_layer(step)

    for h in range(2, len(chunks)):
        relay(h)

    @pl.loop(2, groups)
    def _(step):
        for h, first in enumerate(firsts):
            if h >= 2:
                @pl.when(step == first)
                def _(h=h):
                    await_x(h)

        first_layer(step)

    def await_h(g):
        for d, _, comes, _, _ in ways:
            @pl.when(comes)
            def _(d=d):
                to_h(d, g).wait_recv()

    def to_o(k, g):
        here = pl.ds(pl.multiple_of(g * group, group), group)
        there = pl.ds(pl.multiple_of(c * width + g * group, group), group)
        return pltpu.make_async_remote_copy(
            src_ref=result.at[part(peers[k]), here], dst_ref=out.at[:, there],
            send_sem=o_send.at[k - 1, g], recv_sem=o_recv.at[k - 1, g],
            device_id=(s, peers[k]), device_id_type=MESH)

    def own_o(g):
        here = pl.ds(pl.multiple_of(g * group, group), group)
        there = pl.ds(pl.multiple_of(c * width + g * group, group), group)
        return pltpu.make_async_copy(
            result.at[part(c), here], out.at[:, there], o_local.at[g])

    await_h(0)
    await_edge(1)

    @pl.loop(0, groups)
    def _(g):
        @pl.when(g < groups - 1)
        def _():
            await_h(g + 1)

        @pl.when(g == groups - 1)
        def _():
            await_edge(0)

        layer(hidden, mat2, bias[1], g, finish)
        for k in range(1, nc):
            to_o(k, g).start()
        own_o(g).start()

    for (k, h), copy in to_z.items():
        copy.wait_send()
    for d, sends, _, _, _ in ways:
        @pl.when(sends)
        def _(d=d):
            for k in range(nc):
                for h in range(len(chunks)):
                    to_x[d, k, h].wait_send()

            @pl.loop(0, groups)
            def _(g):
                to_h(d, g).wait_send()
    for d, sends, _, _, _ in planes:
        for t, goes, _, _, _, _ in rims:
            @pl.when(sends & goes)
            def _(d=d, t=t):
                to_e[d, t].wait_send()

    @pl.loop(0, groups)
    def _(g):
        for k in range(1, nc):
            to_o(k, g).wait()
        own_o(g).wait()


def per_device(volume, weight_one, bias_one, weight_two, bias_two):
    own, planes, height, depth = volume.shape
    ns, nc = lax.axis_size("space"), lax.axis_size("chan")
    rows = height // nc
    chans = own * nc
    wide = (rows + 2) * depth
    cuts = len(row_chunks(rows))
    flat = jnp.pad(volume.reshape(own, height * depth), ((0, 0), (depth, depth)))
    dma = pltpu.SemaphoreType.DMA
    any_space = pl.BlockSpec(memory_space=pl.ANY)
    macs = 27 * chans * chans * rows * depth
    result = pl.pallas_call(
        functools.partial(kernel, ns, nc, rows, depth, own),
        out_shape=jax.ShapeDtypeStruct((own, height * depth), BF16),
        in_specs=[any_space] * 5,
        out_specs=any_space,
        scratch_shapes=[
            pltpu.VMEM((3, chans, wide), BF16),
            pltpu.VMEM((3, chans, wide), BF16),
            pltpu.VMEM((chans, rows * depth), BF16),
            pltpu.VMEM(weight_one.shape, BF16),
            pltpu.VMEM(weight_two.shape, BF16),
            pltpu.VMEM((3 * chans, 9 * chans), BF16),
            pltpu.VMEM((3 * chans, 9 * chans), BF16),
            pltpu.VMEM((2, chans, depth), F32),
            pltpu.VMEM((2, 1, chans), F32),
            dma((4,)), dma((cuts,)),
            dma((nc - 1, cuts)), dma((nc - 1, cuts)),
            dma((2, nc, cuts)), dma((2, nc, cuts)),
            dma((2, rows // PAIR)), dma((2, rows // PAIR)),
            dma((3, 2)), dma((3, 2)),
            dma((nc - 1, rows // PAIR)), dma((nc - 1, rows // PAIR)), dma((rows // PAIR,)),
        ],
        compiler_params=pltpu.CompilerParams(
            collective_id=0, has_side_effects=True, vmem_limit_bytes=60 * 2**20),
        cost_estimate=pl.CostEstimate(
            flops=4 * macs, bytes_accessed=4 * 2**20, transcendentals=0),
        name="conv_pair",
    )(flat, weight_one, bias_one.reshape(1, chans), weight_two, bias_two.reshape(1, chans))
    return result.reshape(own, planes, height, depth)


def solution(mesh):
    placed = (P("chan", "space", None, None), P(), P(), P(), P())
    return jax.shard_map(
        per_device,
        mesh=mesh,
        in_specs=placed,
        out_specs=P("chan", "space", None, None),
        check_vma=False,
    )
```
